512 devices in a mesh: half: 2 (over core), face: 8 (over x, y_lo), tile: 32 (over y_hi, z).
Axes of the slice: x: 4, y: 4 (y_hi: 2, y_lo: 2; y = y_hi * 2 + y_lo), z: 16, core: 2. Of those that a mesh axis runs over, the one named last changes fastest.
Arguments:
- state: bfloat16 [2, 16, 32, 4096], P('half', None, 'face', 'tile'), may hold values from -6 to 6
- cotangent: bfloat16 [2, 16, 32, 4096], P('half', None, 'face', 'tile'), may hold values from -6 to 6
- block_peer: int32 [2, 8, 32, 32, 1], P('half', 'face', 'tile'), may hold values from 0 to 31; in each aligned block of 32 rows (0 to 31, 32 to 63, ..., all dimensions but the last counted through in order) at most 2 rows name the same one
- source_start: int32 [2, 8, 32, 32], P('half', 'face', 'tile'), may hold values from 0 to 448
- target_start: int32 [2, 8, 32, 32, 2], P('half', 'face', 'tile'), may hold values from 0 to 448
- interp: bfloat16 [2, 64, 64], P('half'), may hold values from -0.75 to 0.75
- sea_mask: int32 [2, 32, 4096], P('half', 'face', 'tile'), may hold values 0 or 1
- w_first: bfloat16 [2, 9, 1280], P('half'), may hold values from -0.4375 to 0.4375
- w_down: bfloat16 [2, 9, 8192], P('half'), may hold values from -0.25 to 0.25
- w_up: bfloat16 [2, 9, 12288], P('half'), may hold values from -0.15625 to 0.15625
- w_out: bfloat16 [2, 1024], P('half'), may hold values from -0.75 to 0.75
Outputs:
- predicted: bfloat16 [2, 16, 32, 4096], P('half', None, 'face', 'tile')
- grad_first: float32 [2, 9, 1280], P('half')
- grad_down: float32 [2, 9, 8192], P('half')
- grad_up: float32 [2, 9, 12288], P('half')
- grad_out: float32 [2, 1024], P('half')
The draws below stay inside these ranges and needn't reach their ends.
Inputs may be any that keep to these rules, and one draw needn't show every extreme that they name: `block_peer`: of the blocks of one device no more than 2 name the same tile, and in every draw some device has exactly 2 blocks to one tile. `target_start`: entries of slots that no block uses are never read.
All inputs are finite; a program needn't handle non-finite values. No bound on the sum of `sea_mask` on one device may be relied on, other than what follows from the above.
Results may differ from the reference program's by a relative error of at most 0.0082.
Values may be sent and summed in bfloat16 or wider, within the bound.
A program may use at most 64 MiB of HBM per device.

```python
import math
import jax
import jax.numpy as jnp
import numpy as np
from jax import lax

CH = 64
CIN = 16
KC = 4
BS = 64
CAP = 2
NBLK = 32
HT = 4
WT = 128
NR = 32
NC = 4096
N_FACE = 8
N_TILE = 32


def with_ends(entries, rng, least, largest):
    shape = entries.shape
    spot = [jax.random.randint(jax.random.fold_in(rng, axis), (), 0, shape[axis]) for axis in range(len(shape))]
    entries = entries.at[tuple(spot)].set(least)
    longest = shape.index(max(shape))
    spot[longest] = (spot[longest] + 1) % shape[longest]
    return entries.at[tuple(spot)].set(largest)


def block_scale(rng, shape, split, least, largest):
    gain, own = 1.0, jax.random.fold_in(rng, 6)
    for dim, shards_of in split:
        steps = jnp.exp(jax.random.uniform(jax.random.fold_in(own, dim), (shards_of,), jnp.float32, least / len(split), largest / len(split)))
        gain = gain * jnp.repeat(steps, shape[dim] // shards_of).reshape([-1 if axis == dim else 1 for axis in range(len(shape))])
    return gain


def assign_block(stream_key, own, number, rows, count, top, limit, slope):
    ranking = jax.random.permutation(stream_key, count)
    packed, ordinary = load_shares(count, rows * top, limit, slope, True), load_shares(count, rows * top, limit, slope, False)
    places = jnp.arange(count)

    def named(tallies, offset_by):
        used = int((tallies > 0).sum())
        fixed = max(1, used // 4)
        shifted = fixed + (places - fixed + offset_by * (used - fixed)) % max(1, count - fixed)
        return jnp.zeros((count,), jnp.int32).at[ranking[jnp.where(places < fixed, places, shifted)]].set(jnp.asarray(tallies, jnp.int32))

    tallies = jnp.where(number % 4 == 0, named(packed, number // 4), named(ordinary, number - number // 4 - 1))
    mixed = jax.random.permutation(jax.random.fold_in(own, 3), count)
    donor, sink = mixed[0:count // 2 * 2:2], mixed[1:count // 2 * 2:2]
    slack = jnp.minimum(tallies[donor] - 1, limit - tallies[sink]) // 2
    slack = jnp.where((donor == ranking[0]) | (sink == ranking[0]) | (tallies[sink] == 0), 0, jnp.maximum(slack, 0))
    shifted = jax.random.randint(jax.random.fold_in(own, 4), (count // 2,), 0, 1 << 20) % (slack + 1)
    tallies = tallies.at[donor].add(-shifted).at[sink].add(shifted)
    labels = jnp.searchsorted(jnp.cumsum(tallies), jnp.arange(rows * top), side="right").astype(jnp.int32)
    listing = labels.reshape(top, rows).T
    listing = listing[jax.random.permutation(jax.random.fold_in(own, 1), rows)]
    offset_by = jax.random.randint(jax.random.fold_in(own, 2), (rows, 1), 0, top)
    return jnp.take_along_axis(listing, (jnp.arange(top)[None, :] + offset_by) % top, axis=1)


def load_shares(number_of, total, bound, slope, full):
    portions = [(1 << 20) // math.isqrt(grade ** slope) + 1 for grade in range(1, number_of + 1)]
    largest = bound if full else min(bound, max(-(-total // number_of), total * portions[0] // sum(portions)))
    least = 1 if total - largest >= number_of - 1 else 0
    given, surplus = [largest] + [least] * (number_of - 1), total - largest - least * (number_of - 1)
    while surplus > 0:
        candidates = [i for i in range(1, number_of) if given[i] < largest] or [i for i in range(1, number_of) if given[i] < bound]
        mass, left = sum([portions[i] for i in candidates]), surplus
        for i in candidates:
            extra = min(bound - given[i], max(1, left * portions[i] // mass), surplus)
            given[i] = given[i] + extra
            surplus = surplus - extra
    return np.array(given)


def bell_draw(stream_key, shape, width, most, shards=(), kind=jnp.bfloat16):
    loudness = block_scale(stream_key, shape, shards, -0.22, 0.18) if shards else 1.0
    drawn = jax.random.normal(stream_key, shape, jnp.float32) * width * loudness
    return jnp.minimum(jnp.maximum(drawn, -most), most).astype(kind)


def setup_inputs(seed: int = 0) -> dict:
    splits = jax.random.split(jax.random.key(seed), 12)
    state = bell_draw(splits[0], (2, CIN, NR, NC), 1.0, 6.0, ((0, 2), (2, 8), (3, 32)))
    cotangent = bell_draw(splits[1], (2, CIN, NR, NC), 1.0, 6.0, ((0, 2), (2, 8), (3, 32)))
    block_peer_keys = jax.random.split(jax.random.fold_in(splits[2], 1), 2 * N_FACE * N_TILE * NBLK // NBLK)
    block_peer_turns = jax.random.permutation(jax.random.fold_in(splits[2], 3), 2 * N_FACE * N_TILE * NBLK // NBLK)
    block_peer = jax.vmap(lambda own, number: assign_block(jax.random.fold_in(splits[2], 2), own, number, NBLK, N_TILE, 1, CAP, 2))(block_peer_keys, block_peer_turns).reshape((2, N_FACE, N_TILE, NBLK, 1))
    source_start = with_ends(jax.random.randint(splits[3], (2, N_FACE, N_TILE, NBLK), 0, HT * WT - BS + 1), jax.random.fold_in(splits[3], 1), 0, HT * WT - BS).astype(jnp.int32)
    target_start = with_ends(jax.random.randint(splits[4], (2, N_FACE, N_TILE, N_TILE, CAP), 0, HT * WT - BS + 1), jax.random.fold_in(splits[4], 1), 0, HT * WT - BS).astype(jnp.int32)
    interp = bell_draw(splits[5], (2, BS, BS), BS ** -0.5, 0.75, ((0, 2),))
    sea_mask = with_ends((jax.random.randint(splits[6], (2, NR, NC), 0, 3) < 2).astype(jnp.int32), jax.random.fold_in(splits[6], 1), 0, 1)
    w_first = bell_draw(splits[7], (2, 9, CH * (CIN + KC)), (9 * (CIN + KC)) ** -0.5, 0.4375, ((0, 2),))
    w_down = bell_draw(splits[8], (2, 9, 2 * CH * CH), (9 * CH) ** -0.5, 0.25, ((0, 2),))
    w_up = bell_draw(splits[9], (2, 9, CH * 3 * CH), (9 * 3 * CH) ** -0.5, 0.15625, ((0, 2),))
    w_out = bell_draw(splits[10], (2, CIN * CH), CH ** -0.5, 0.75, ((0, 2),))
    return {"state": state, "cotangent": cotangent, "block_peer": block_peer, "source_start": source_start, "target_start": target_start, "interp": interp, "sea_mask": sea_mask, "w_first": w_first, "w_down": w_down, "w_up": w_up, "w_out": w_out}


GELU_C = math.sqrt(2.0 / math.pi)

def gelu_value(pre):
    inner = jnp.tanh(GELU_C * (pre + 0.044715 * pre * pre * pre))
    return 0.5 * pre * (1.0 + inner)

def gelu_slope(pre):
    inner = jnp.tanh(GELU_C * (pre + 0.044715 * pre * pre * pre))
    return 0.5 * (1.0 + inner) + 0.5 * pre * (1.0 - inner * inner) * GELU_C * (1.0 + 3.0 * 0.044715 * pre * pre)

def pad_grid(field):
    return jnp.pad(field, ((0, 0), (1, 1), (1, 1)))

def convolve(padded, weight, height, breadth):
    chans = padded.shape[0]
    result = jnp.zeros((weight.shape[1], height * breadth), jnp.float32)
    for kernel_pos in range(9):
        row_shift, col_shift = (kernel_pos // 3, kernel_pos % 3)
        window = padded[:, row_shift:row_shift + height, col_shift:col_shift + breadth].reshape(chans, -1)
        result = result + jnp.dot(weight[kernel_pos], window, preferred_element_type=jnp.float32)
    return result

def convolve_adjoint(padded, weight, height, breadth):
    chans = padded.shape[0]
    result = jnp.zeros((weight.shape[2], height * breadth), jnp.float32)
    for kernel_pos in range(9):
        row_shift, col_shift = (kernel_pos // 3, kernel_pos % 3)
        window = padded[:, 2 - row_shift:2 - row_shift + height, 2 - col_shift:2 - col_shift + breadth].reshape(chans, -1)
        result = result + lax.dot_general(weight[kernel_pos], window, (((0,), (0,)), ((), ())), preferred_element_type=jnp.float32)
    return result

def weight_grad(delta, padded, height, breadth):
    chans = padded.shape[0]
    parts = []
    for kernel_pos in range(9):
        row_shift, col_shift = (kernel_pos // 3, kernel_pos % 3)
        window = padded[:, row_shift:row_shift + height, col_shift:col_shift + breadth].reshape(chans, -1)
        parts.append(lax.dot_general(delta, window, (((1,), (1,)), ((), ())), preferred_element_type=jnp.float32))
    return jnp.stack(parts)

def pool_pairs(field):
    chans, height, breadth = field.shape
    return field.astype(jnp.float32).reshape(chans, height // 2, 2, breadth // 2, 2).mean(axis=(2, 4)).astype(jnp.bfloat16)

def widen(field):
    return jnp.repeat(jnp.repeat(field, 2, axis=1), 2, axis=2)

def group_sum(field):
    chans, height, breadth = field.shape
    return field.reshape(chans, height // 2, 2, breadth // 2, 2).sum(axis=(2, 4))

def couple(state, block_peer, source_start, target_start, interp, sea_mask, comp):
    src = 1 - comp
    tile_cells = HT * WT
    export = state[src, :KC].reshape(KC, N_FACE, HT, N_TILE, WT).transpose(1, 3, 0, 2, 4).reshape(N_FACE, N_TILE, KC, tile_cells)
    offsets = jnp.arange(BS, dtype=jnp.int32)
    source_idx = source_start[src][..., None] + offsets
    values = jnp.take_along_axis(export[:, :, None, :, :], source_idx[:, :, :, None, :], axis=4)
    moved = jnp.einsum('ftbkx,xy->ftbky', values.astype(jnp.float32), interp[comp].astype(jnp.float32))
    peer_ids = block_peer[src][..., 0]
    onehot = (peer_ids[..., None] == jnp.arange(N_TILE, dtype=jnp.int32)).astype(jnp.int32)
    slot_ids = lax.optimization_barrier(jnp.sum(jnp.cumsum(onehot, axis=2) * onehot, axis=-1)) - 1
    face_ids = jnp.arange(N_FACE, dtype=jnp.int32)[:, None, None]
    tile_ids = jnp.arange(N_TILE, dtype=jnp.int32)[None, :, None]
    landing = target_start[comp][face_ids, peer_ids, tile_ids, slot_ids]
    target_idx = landing[..., None] + offsets
    forcing_sum = jnp.zeros((N_FACE, N_TILE, KC, tile_cells), jnp.float32)
    forcing_sum = forcing_sum.at[face_ids[..., None], peer_ids[..., None], :, target_idx].add(jnp.transpose(moved, (0, 1, 2, 4, 3)))
    mask_tiles = sea_mask[comp].reshape(N_FACE, HT, N_TILE, WT).transpose(0, 2, 1, 3).reshape(N_FACE, N_TILE, tile_cells)
    forcing = (forcing_sum * mask_tiles[:, :, None, :].astype(jnp.float32)).astype(jnp.bfloat16)
    return forcing.reshape(N_FACE, N_TILE, KC, HT, WT).transpose(2, 0, 3, 1, 4).reshape(KC, NR, NC)

def reference(state, cotangent, block_peer, source_start, target_start, interp, sea_mask, w_first, w_down, w_up, w_out):
    scale = 1.0 / math.sqrt(NR * NC)
    outputs = [[], [], [], [], []]
    for comp in range(2):
        first_w = w_first[comp].reshape(9, CH, CIN + KC)
        down_w = w_down[comp].reshape(9, 2 * CH, CH)
        up_w = w_up[comp].reshape(9, CH, 3 * CH)
        out_w = w_out[comp].reshape(CIN, CH)
        forcing = couple(state, block_peer, source_start, target_start, interp, sea_mask, comp)
        lifted_pad = pad_grid(jnp.concatenate([state[comp], forcing], axis=0))
        pre_one = convolve(lifted_pad, first_w, NR, NC)
        hidden_one = gelu_value(pre_one).astype(jnp.bfloat16).reshape(CH, NR, NC)
        pooled_pad = pad_grid(pool_pairs(hidden_one))
        pre_two = convolve(pooled_pad, down_w, NR // 2, NC // 2)
        hidden_two = gelu_value(pre_two).astype(jnp.bfloat16).reshape(2 * CH, NR // 2, NC // 2)
        joined_pad = pad_grid(jnp.concatenate([hidden_one, widen(hidden_two)], axis=0))
        pre_three = convolve(joined_pad, up_w, NR, NC)
        hidden_three = gelu_value(pre_three).astype(jnp.bfloat16)
        base = state[comp].reshape(CIN, -1).astype(jnp.float32)
        predicted = (base + jnp.dot(out_w, hidden_three, preferred_element_type=jnp.float32)).astype(jnp.bfloat16)
        upstream = cotangent[comp].reshape(CIN, -1)
        grad_out = lax.dot_general(upstream, hidden_three, (((1,), (1,)), ((), ())), preferred_element_type=jnp.float32)
        back_three = lax.dot_general(out_w, upstream, (((0,), (0,)), ((), ())), preferred_element_type=jnp.float32)
        d_three = (back_three * gelu_slope(pre_three)).astype(jnp.bfloat16)
        grad_up = weight_grad(d_three, joined_pad, NR, NC)
        d_join = convolve_adjoint(pad_grid(d_three.reshape(CH, NR, NC)), up_w, NR, NC)
        back_two = group_sum(d_join[CH:].reshape(2 * CH, NR, NC)).reshape(2 * CH, -1)
        d_two = (back_two * gelu_slope(pre_two)).astype(jnp.bfloat16)
        grad_down = weight_grad(d_two, pooled_pad, NR // 2, NC // 2)
        d_pool = convolve_adjoint(pad_grid(d_two.reshape(2 * CH, NR // 2, NC // 2)), down_w, NR // 2, NC // 2)
        back_one = d_join[:CH] + 0.25 * widen(d_pool.reshape(CH, NR // 2, NC // 2)).reshape(CH, -1)
        d_one = (back_one * gelu_slope(pre_one)).astype(jnp.bfloat16)
        grad_first = weight_grad(d_one, lifted_pad, NR, NC)
        outputs[0].append(predicted.reshape(CIN, NR, NC))
        outputs[1].append((grad_first * scale).reshape(9, -1))
        outputs[2].append((grad_down * scale).reshape(9, -1))
        outputs[3].append((grad_up * scale).reshape(9, -1))
        outputs[4].append((grad_out * scale).reshape(-1))
    return (jnp.stack(outputs[0]), jnp.stack(outputs[1]), jnp.stack(outputs[2]), jnp.stack(outputs[3]), jnp.stack(outputs[4]))
```

```python
import functools
import math

import jax
import jax.numpy as jnp
import numpy as np
from jax import lax
from jax.experimental import pallas as pl
from jax.experimental.pallas import tpu as pltpu
from jax.sharding import PartitionSpec as P

CH = 64
CIN = 16
KC = 4
BS = 64
LANES = 128
GELU_C = math.sqrt(2.0 / math.pi)
BF = jnp.bfloat16
F32 = jnp.float32
MESH = pl.DeviceIdType.MESH
DIRS = [(-1, 0), (1, 0), (0, -1), (0, 1), (-1, -1), (-1, 1), (1, -1), (1, 1)]
OPP = [DIRS.index((-a, -b)) for a, b in DIRS]
N_EX = 5
EX_CH = (32, 128, 128, 64, 128)


def gelu_pair(pre):
    inner = jnp.tanh(GELU_C * (pre + 0.044715 * pre * pre * pre))
    value = 0.5 * pre * (1.0 + inner)
    slope = 0.5 * (1.0 + inner) + 0.5 * pre * (1.0 - inner * inner) * GELU_C * (
        1.0 + 3.0 * 0.044715 * pre * pre
    )
    return value, slope


def roll(x, shift):
    return pltpu.roll(x, shift % LANES, axis=1)


def lanes_of(rows):
    return lax.broadcasted_iota(jnp.int32, (rows, LANES), 1)


def barrel(x, amount, right):
    for bit in range(7):
        step = 1 << bit
        moved = roll(x, step if right else LANES - step)
        x = jnp.where((amount & step) != 0, moved, x)
    return x


def pair_sum(x):
    even = (lanes_of(x.shape[0]) & 1) == 0
    return x + jnp.where(even, roll(x, -1), roll(x, 1))


def edge_tables():
    pick_fine = np.zeros((16, 4 * LANES), np.float32)
    pick_coarse = np.zeros((16, 2 * LANES), np.float32)
    for base, lane in ((0, LANES - 1), (8, 0)):
        for j, row in enumerate((3, 0, 1, 2, 3, 0)):
            pick_fine[base + j, row * LANES + lane] = 1
            pick_coarse[base + j, (row // 2) * LANES + lane] = 1
    place_fine = np.zeros((3, 16, LANES), np.float32)
    place_coarse = np.zeros((3, 16, LANES), np.float32)
    for a in range(3):
        for base, start in ((0, 0), (8, 64)):
            for r in range(4):
                place_fine[a, base + r + a, start + r] = 1
            for r in range(2):
                place_coarse[a, base + (0, 1, 3, 5)[r + a], start + r] = 1
    return pick_fine, pick_coarse, place_fine, place_coarse


def conv_rows(weight, x_ref, outs, rows, step):
    z = jnp.dot(weight, x_ref[...], preferred_element_type=F32)
    lane = lanes_of(outs)
    halo_left = z[:outs, rows * LANES :]
    halo_right = z[2 * outs :, rows * LANES :]
    result = []
    for r in range(rows):
        at = slice(r * LANES, (r + 1) * LANES)
        left = jnp.where(lane < step, halo_left[:, r : r + 1], roll(z[:outs, at], step))
        right = jnp.where(
            lane >= LANES - step, halo_right[:, 64 + r : 65 + r], roll(z[2 * outs :, at], -step)
        )
        result.append(z[outs : 2 * outs, at] + left + right)
    return result


def weight_grad(delta_rows, x_ref, step):
    outs = delta_rows[0].shape[0]
    lane = lanes_of(outs)
    keep = (lane & (step - 1)) == 0
    zero = jnp.zeros((outs, LANES), F32)
    first, middle, last = [], [], []
    halo_left, halo_right = zero, zero
    for r, delta in enumerate(delta_rows):
        first.append(jnp.where(keep & (lane < LANES - step), roll(delta, -step), 0.0))
        middle.append(jnp.where(keep, delta, 0.0))
        last.append(jnp.where(keep & (lane >= step), roll(delta, step), 0.0))
        halo_left = jnp.where(lane == r, delta[:, 0:1], halo_left)
        halo_right = jnp.where(lane == 64 + r, delta[:, LANES - 1 : LANES], halo_right)
    parts = [first + [halo_left], middle + [zero], last + [halo_right]]
    stacked = jnp.concatenate(
        [jnp.concatenate(part, axis=1).astype(BF) for part in parts], axis=0
    )
    return lax.dot_general(
        stacked, x_ref[...], (((1,), (1,)), ((), ())), preferred_element_type=F32
    )


def kernel(
    nf,
    nt,
    na,
    nb,
    state_ref,
    cot_ref,
    peer_row_ref,
    peer_col_ref,
    src_ref,
    tgt_ref,
    interp_ref,
    sea_ref,
    a1_ref,
    a2_ref,
    a3_ref,
    b2_ref,
    b3_ref,
    wo_ref,
    wot_ref,
    pickf_ref,
    pickc_ref,
    placef_ref,
    placec_ref,
    pred_ref,
    ga_ref,
    gb_ref,
    outbox,
    inbox,
    row_send,
    row_recv,
    edge_send,
    edge_recv,
    x1,
    x2,
    x3,
    xd3,
    xd2,
    send_a,
    recv_a,
    part_a,
    zrecv_a,
    done_a,
    all_a,
    send_b,
    recv_b,
    part_b,
    zrecv_b,
    done_b,
    all_b,
    box_ssem,
    box_rsem,
    ex_ssem,
    ex_rsem,
    xy_ssem,
    xy_rsem,
    zs_ssem,
    zs_rsem,
    zg_ssem,
    zg_rsem,
    gx_ssem,
    gx_rsem,
):
    half = lax.axis_index("half")
    face = lax.axis_index("face")
    tile = lax.axis_index("tile")
    nz = nt // 2
    nxy = nf * 2
    y_hi = tile // nz
    z = tile % nz
    me_xy = face * 2 + y_hi

    def xy_peer(k):
        other = (me_xy + k) % nxy
        return other, {"face": other // 2, "tile": (other % 2) * nz + z}

    def z_peer(k):
        other = (z + k) % nz
        return other, {"tile": y_hi * nz + other}

    def box_peer(k):
        other = (tile + k) % nt
        return other, {"half": 1 - half, "tile": other}

    def neighbour(d):
        df, dt = DIRS[d]
        ok = (face + df >= 0) & (face + df < nf) & (tile + dt >= 0) & (tile + dt < nt)
        return ok, {"face": face + df, "tile": tile + dt}

    row_recv[...] = jnp.zeros_like(row_recv)
    edge_recv[...] = jnp.zeros_like(edge_recv)
    edge_send[...] = jnp.zeros_like(edge_send)

    barrier = pltpu.get_barrier_semaphore()

    def greet(peer, count):
        def body(k, carry):
            pl.semaphore_signal(barrier, inc=1, device_id=peer(k)[1], device_id_type=MESH)
            return carry

        lax.fori_loop(count[0], count[1], body, 0)

    greet(box_peer, (0, nt))
    greet(xy_peer, (1, nxy))
    greet(z_peer, (1, nz))
    expected = nt + nxy - 1 + nz - 1
    for d in range(8):
        ok, device = neighbour(d)
        expected = expected + ok.astype(jnp.int32)

        @pl.when(ok)
        def _(device=device):
            pl.semaphore_signal(barrier, inc=1, device_id=device, device_id_type=MESH)

    rows = 2 * nt * KC
    nblk = src_ref.shape[1]
    peer_row = peer_row_ref[...]
    same = peer_col_ref[...] == peer_row
    earlier = lax.broadcasted_iota(jnp.int32, (nblk, nblk), 0) < lax.broadcasted_iota(
        jnp.int32, (nblk, nblk), 1
    )
    rank = jnp.sum(jnp.where(same & earlier, 1.0, 0.0), axis=0, keepdims=True)
    row_id = lax.broadcasted_iota(jnp.int32, (rows, nblk), 0)
    slot = (row_id // (nt * KC)).astype(F32)
    match = ((row_id // KC) % nt == peer_row) & (slot == rank)
    used = jnp.sum(jnp.where(match, 1.0, 0.0), axis=1, keepdims=True)
    start = jnp.sum(
        jnp.where(match, src_ref[...].astype(F32), 0.0), axis=1, keepdims=True
    ).astype(jnp.int32)
    start = jnp.broadcast_to(start, (rows, LANES))
    lane = lanes_of(rows)
    sub8 = lax.broadcasted_iota(jnp.int32, (8, LANES), 0)
    shift = start & (LANES - 1)
    from_tile = (start >> 7) + (lane < shift).astype(jnp.int32)
    window = jnp.zeros((rows, LANES), F32)
    for q in range(4):
        head = state_ref[:, q * LANES : (q + 1) * LANES].astype(F32)[0:8]
        head = jnp.where(sub8 < KC, head, pltpu.roll(head, 4, axis=0))
        window = jnp.where(
            from_tile == q, jnp.concatenate([head] * (rows // 8), axis=0), window
        )
    window = barrel(window, shift, False)
    window = jnp.where((lane < BS) & (used > 0.0), window, 0.0)
    packed = window[: rows // 2] + roll(window[rows // 2 :], BS)
    for p in range(nt):
        outbox[p] = packed[p * KC : (p + 1) * KC]

    pl.semaphore_wait(barrier, expected)

    def box_copy(k):
        other, device = box_peer(k)
        return pltpu.make_async_remote_copy(
            src_ref=outbox.at[other],
            dst_ref=inbox.at[tile],
            send_sem=box_ssem.at[k],
            recv_sem=box_rsem.at[tile],
            device_id=device,
            device_id_type=MESH,
        )

    def box_arrival(k):
        other, device = box_peer(k)
        return pltpu.make_async_remote_copy(
            src_ref=outbox.at[other],
            dst_ref=inbox.at[other],
            send_sem=box_ssem.at[k],
            recv_sem=box_rsem.at[other],
            device_id=device,
            device_id_type=MESH,
        )

    def each(low, high, act):
        def body(k, carry):
            act(k)
            return carry

        lax.fori_loop(low, high, body, 0)

    each(0, nt, lambda k: box_copy(k).start())

    def ex_copy(e, d, arrival):
        ok, device = neighbour(d)
        at = d if arrival else OPP[d]
        if d < 2:
            src = row_send.at[e, d, 0 : EX_CH[e]]
            dst = row_recv.at[e, at, 0 : EX_CH[e]]
        else:
            src = edge_send.at[e]
            dst = edge_recv.at[e, at - 2]
        return ok, pltpu.make_async_remote_copy(
            src_ref=src,
            dst_ref=dst,
            send_sem=ex_ssem.at[e, d],
            recv_sem=ex_rsem.at[e, at],
            device_id=device,
            device_id_type=MESH,
        )

    def ex_start(e):
        for d in range(8):
            ok, copy = ex_copy(e, d, False)
            pl.when(ok)(copy.start)

    def ex_wait(e):
        for d in range(8):
            ok, copy = ex_copy(e, d, True)

            @pl.when(ok)
            def _(copy=copy):
                copy.wait_recv()
                copy.wait_send()

    def pick(table_ref, field):
        return lax.dot_general(
            table_ref[...], field, (((1,), (1,)), ((), ())), preferred_element_type=F32
        ).astype(BF)

    sub16 = lax.broadcasted_iota(jnp.int32, (16, LANES), 0)
    takes = {
        2: (sub16 >= 1) & (sub16 <= 4),
        3: (sub16 >= 9) & (sub16 <= 12),
        4: sub16 == 0,
        5: sub16 == 8,
        6: sub16 == 5,
        7: sub16 == 13,
    }

    def halo_columns(e):
        held = jnp.zeros((16, LANES), F32)
        for d in range(2, 8):
            held = jnp.where(takes[d], edge_recv[e, d - 2].astype(F32), held)
        return held.T

    def place(columns, table_ref, a):
        return jnp.dot(
            columns.astype(BF), table_ref[a], preferred_element_type=F32
        ).astype(BF)

    def fill_centre(x_ref, chans, offset, total, field_rows):
        count = len(field_rows)
        for a in range(3):
            for r in range(count):
                if 1 <= r + a <= count:
                    x_ref[
                        a * total + offset : a * total + offset + chans,
                        r * LANES : (r + 1) * LANES,
                    ] = field_rows[r + a - 1]

    def fill_halo(x_ref, chans, offset, total, count, above, below, columns, table_ref):
        x_ref[offset : offset + chans, 0:LANES] = above
        x_ref[
            2 * total + offset : 2 * total + offset + chans, (count - 1) * LANES : count * LANES
        ] = below
        for a in range(3):
            x_ref[
                a * total + offset : a * total + offset + chans, count * LANES :
            ] = place(columns, table_ref, a)

    def xy_copy(g, k, arrival):
        other, device = xy_peer(k)
        send, recv, m = ((send_a, recv_a, 16 * na), (send_b, recv_b, 16 * nb))[g]
        at = other if arrival else me_xy
        return pltpu.make_async_remote_copy(
            src_ref=send.at[pl.ds(pl.multiple_of(other * m, 16), m)],
            dst_ref=recv.at[at],
            send_sem=xy_ssem.at[g, k],
            recv_sem=xy_rsem.at[g, at],
            device_id=device,
            device_id_type=MESH,
        )

    groups = (
        (na, send_a, recv_a, part_a, zrecv_a, done_a, all_a, 0),
        (nb, send_b, recv_b, part_b, zrecv_b, done_b, all_b, 2),
    )

    def xy_start(g):
        each(1, nxy, lambda k: xy_copy(g, k, False).start())

    def z_owner(g, q):
        return (4 * q + groups[g][7]) % nz

    def zs_copy(g, q, source):
        n, send, recv, part, zrecv, done, full, first = groups[g]
        base = 0 if g == 0 else na
        return pltpu.make_async_remote_copy(
            src_ref=part.at[16 * q : 16 * q + 16],
            dst_ref=zrecv.at[q, source],
            send_sem=zs_ssem.at[base + q],
            recv_sem=zs_rsem.at[base + q, source],
            device_id={"tile": y_hi * nz + z_owner(g, q)},
            device_id_type=MESH,
        )

    def zg_copy(g, q, k):
        n, send, recv, part, zrecv, done, full, first = groups[g]
        base = 0 if g == 0 else na
        return pltpu.make_async_remote_copy(
            src_ref=done.at[16 * q : 16 * q + 16],
            dst_ref=done.at[16 * q : 16 * q + 16],
            send_sem=zg_ssem.at[base + q, k],
            recv_sem=zg_rsem.at[base + q],
            device_id=z_peer(k)[1],
            device_id_type=MESH,
        )

    def gx_copy(g, k, arrival):
        other, device = xy_peer(k)
        n, send, recv, part, zrecv, done, full, first = groups[g]
        m = 16 * n
        at = other if arrival else me_xy
        return pltpu.make_async_remote_copy(
            src_ref=done,
            dst_ref=full.at[pl.ds(pl.multiple_of(at * m, 16), m)],
            send_sem=gx_ssem.at[g, k],
            recv_sem=gx_rsem.at[g, at],
            device_id=device,
            device_id_type=MESH,
        )

    def stage_xy_to_z(g):
        n, send, recv, part, zrecv, done, full, first = groups[g]
        m = 16 * n
        total = send[pl.ds(pl.multiple_of(me_xy * m, 16), m), :].astype(F32)
        each(1, nxy, lambda k: xy_copy(g, k, True).wait_recv())
        recv[me_xy] = jnp.zeros((m, LANES), BF)
        for j in range(nxy):
            total = total + recv[j].astype(F32)
        part[...] = total.astype(BF)
        for q in range(n):

            @pl.when(z != z_owner(g, q))
            def _(q=q):
                zs_copy(g, q, z).start()

    def stage_z_reduce(g):
        n, send, recv, part, zrecv, done, full, first = groups[g]
        for q in range(n):

            @pl.when(z == z_owner(g, q))
            def _(q=q):
                each(1, nz, lambda k: zs_copy(g, q, z_peer(k)[0]).wait_recv())
                zrecv[q, z] = part[16 * q : 16 * q + 16]
                total = jnp.zeros((16, LANES), F32)
                for j in range(nz):
                    total = total + zrecv[q, j].astype(F32)
                done[16 * q : 16 * q + 16] = total.astype(BF)
                each(1, nz, lambda k: zg_copy(g, q, k).start())

    def stage_z_to_xy(g):
        n, send, recv, part, zrecv, done, full, first = groups[g]
        for q in range(n):

            @pl.when(z != z_owner(g, q))
            def _(q=q):
                zg_copy(g, q, 1).wait_recv()

        each(1, nxy, lambda k: gx_copy(g, k, False).start())

    def stage_finish(g, out_ref):
        n, send, recv, part, zrecv, done, full, first = groups[g]
        m = 16 * n
        each(1, nxy, lambda k: gx_copy(g, k, True).wait_recv())
        full[pl.ds(pl.multiple_of(me_xy * m, 16), m), :] = done[...]
        scale = 1.0 / math.sqrt(nf * 4 * nt * LANES)
        out_ref[...] = full[...].astype(F32) * scale
        each(1, nxy, lambda k: xy_copy(g, k, False).wait_send())
        for q in range(n):

            @pl.when(z != z_owner(g, q))
            def _(q=q):
                zs_copy(g, q, z).wait_send()

            @pl.when(z == z_owner(g, q))
            def _(q=q):
                each(1, nz, lambda k: zg_copy(g, q, k).wait_send())

        each(1, nxy, lambda k: gx_copy(g, k, False).wait_send())

    target = jnp.broadcast_to(tgt_ref[...], (rows, LANES))
    shift_in = target & (LANES - 1)
    to_tile = (target >> 7) + (lane < shift_in).astype(jnp.int32)
    each(0, nt, lambda k: box_arrival(k).wait_recv())
    arrived = jnp.concatenate([inbox[p] for p in range(nt)], axis=0)
    moved = jnp.dot(arrived.astype(BF), interp_ref[...], preferred_element_type=F32)
    lane_half = lanes_of(rows // 2)
    moved = jnp.concatenate(
        [
            jnp.where(lane_half < BS, moved, 0.0),
            roll(jnp.where(lane_half >= BS, moved, 0.0), BS),
        ],
        axis=0,
    )
    moved = barrel(moved, shift_in, True)
    lifted = []
    for q in range(4):
        chosen = jnp.where(to_tile == q, moved, 0.0)
        total = chosen[0:8]
        for i in range(1, rows // 8):
            total = total + chosen[8 * i : 8 * i + 8]
        total = total + pltpu.roll(total, 4, axis=0)
        total = total * sea_ref[q : q + 1, :].astype(F32)
        forcing = jnp.concatenate(
            [jnp.where(sub8 < KC, total, 0.0), jnp.zeros((8, LANES), F32)], axis=0
        ).astype(BF)
        lifted.append(
            jnp.concatenate([state_ref[:, q * LANES : (q + 1) * LANES], forcing], axis=0)
        )

    row_send[0, 0, 0:32] = lifted[0]
    row_send[0, 1, 0:32] = lifted[3]
    edge_send[0, :, 0:32] = pick(pickf_ref, jnp.concatenate(lifted, axis=1))
    ex_start(0)
    fill_centre(x1, 32, 0, 32, lifted)
    ex_wait(0)
    columns = halo_columns(0)[0:32]
    fill_halo(
        x1, 32, 0, 32, 4, row_recv[0, 0, 0:32], row_recv[0, 1, 0:32], columns, placef_ref
    )
    pre = conv_rows(a1_ref[...], x1, CH, 4, 1)
    hidden_one, slope_one = [], []
    for r in range(4):
        value, slope = gelu_pair(pre[r])
        hidden_one.append(value.astype(BF))
        slope_one.append(slope)
    pooled = [
        (
            pair_sum(hidden_one[2 * r].astype(F32) + hidden_one[2 * r + 1].astype(F32)) * 0.25
        ).astype(BF)
        for r in range(2)
    ]

    for at, fine, coarse in ((0, 0, 0), (1, 3, 1)):
        row_send[1, at, 0:CH] = hidden_one[fine]
        row_send[1, at, CH : 2 * CH] = pooled[coarse]
    edge_send[1] = jnp.concatenate(
        [
            pick(pickf_ref, jnp.concatenate(hidden_one, axis=1)),
            pick(pickc_ref, jnp.concatenate(pooled, axis=1)),
        ],
        axis=1,
    )
    ex_start(1)
    fill_centre(x3, CH, 0, 3 * CH, hidden_one)
    fill_centre(x2, CH, 0, CH, pooled)
    ex_wait(1)
    columns = halo_columns(1)
    fill_halo(
        x2,
        CH,
        0,
        CH,
        2,
        row_recv[1, 0, CH : 2 * CH],
        row_recv[1, 1, CH : 2 * CH],
        columns[CH : 2 * CH],
        placec_ref,
    )
    pre = conv_rows(a2_ref[...], x2, 2 * CH, 2, 2)
    hidden_two, slope_two = [], []
    for r in range(2):
        value, slope = gelu_pair(pre[r])
        hidden_two.append(value.astype(BF))
        slope_two.append(slope)

    row_send[2, 0] = hidden_two[0]
    row_send[2, 1] = hidden_two[1]
    edge_send[2] = pick(pickc_ref, jnp.concatenate(hidden_two, axis=1))
    ex_start(2)
    fill_halo(
        x3, CH, 0, 3 * CH, 4, row_recv[1, 0, 0:CH], row_recv[1, 1, 0:CH], columns[0:CH], placef_ref
    )
    fill_centre(x3, 2 * CH, CH, 3 * CH, [hidden_two[r // 2] for r in range(4)])
    back_three = jnp.dot(wot_ref[...], cot_ref[...], preferred_element_type=F32)
    ex_wait(2)
    columns = halo_columns(2)
    fill_halo(
        x3, 2 * CH, CH, 3 * CH, 4, row_recv[2, 0], row_recv[2, 1], columns, placef_ref
    )
    pre = conv_rows(a3_ref[...], x3, CH, 4, 1)
    hidden_three, delta_three = [], []
    for r in range(4):
        value, slope = gelu_pair(pre[r])
        hidden_three.append(value.astype(BF))
        delta_three.append(
            (back_three[:, r * LANES : (r + 1) * LANES] * slope).astype(BF)
        )

    row_send[3, 0, 0:CH] = delta_three[0]
    row_send[3, 1, 0:CH] = delta_three[3]
    edge_send[3, :, 0:CH] = pick(pickf_ref, jnp.concatenate(delta_three, axis=1))
    ex_start(3)
    fill_centre(xd3, CH, 0, CH, delta_three)
    flat_three = jnp.concatenate(hidden_three, axis=1)
    pred_ref[...] = (
        state_ref[...].astype(F32)
        + jnp.dot(wo_ref[...], flat_three, preferred_element_type=F32)
    ).astype(BF)
    grad_out = lax.dot_general(
        cot_ref[...], flat_three, (((1,), (1,)), ((), ())), preferred_element_type=F32
    )
    grad_up = weight_grad([d.astype(F32) for d in delta_three], x3, 1)
    for block in range(4):
        send_a[192 * block : 192 * block + 192] = grad_up[
            :, block * LANES : (block + 1) * LANES
        ].astype(BF)
    send_a[768:864] = jnp.concatenate([grad_up[0:96, 512:576], grad_up[96:192, 512:576]], axis=1).astype(BF)
    send_a[864:880] = jnp.concatenate([grad_out, jnp.zeros((16, 64), F32)], axis=1).astype(BF)
    if 16 * na * nxy > 880:
        send_a[880:] = jnp.zeros((16 * na * nxy - 880, LANES), BF)
    xy_start(0)
    ex_wait(3)
    columns = halo_columns(3)[0:CH]
    fill_halo(
        xd3, CH, 0, CH, 4, row_recv[3, 0, 0:CH], row_recv[3, 1, 0:CH], columns, placef_ref
    )
    join = conv_rows(b3_ref[...], xd3, 3 * CH, 4, 1)
    delta_two = [
        (pair_sum(join[2 * r][CH:] + join[2 * r + 1][CH:]) * slope_two[r]).astype(BF)
        for r in range(2)
    ]

    row_send[4, 0] = delta_two[0]
    row_send[4, 1] = delta_two[1]
    edge_send[4] = pick(pickc_ref, jnp.concatenate(delta_two, axis=1))
    ex_start(4)
    fill_centre(xd2, 2 * CH, 0, 2 * CH, delta_two)
    grad_down = weight_grad([d.astype(F32) for d in delta_two], x2, 2)
    send_b[0:384] = grad_down[:, 0:LANES].astype(BF)
    send_b[384:576] = jnp.concatenate([grad_down[0:192, 128:192], grad_down[192:384, 128:192]], axis=1).astype(BF)
    ex_wait(4)
    columns = halo_columns(4)
    fill_halo(
        xd2, 2 * CH, 0, 2 * CH, 2, row_recv[4, 0], row_recv[4, 1], columns, placec_ref
    )
    d_pool = conv_rows(b2_ref[...], xd2, CH, 2, 2)
    delta_one = [
        ((join[r][0:CH] + 0.25 * d_pool[r // 2]) * slope_one[r]).astype(BF).astype(F32)
        for r in range(4)
    ]
    grad_first = weight_grad(delta_one, x1, 1)
    send_b[576:768] = jnp.concatenate([grad_first, jnp.zeros((192, 32), F32)], axis=1).astype(BF)
    if 16 * nb * nxy > 768:
        send_b[768:] = jnp.zeros((16 * nb * nxy - 768, LANES), BF)
    xy_start(1)
    stage_xy_to_z(0)
    stage_xy_to_z(1)
    stage_z_reduce(0)
    stage_z_reduce(1)
    stage_z_to_xy(0)
    stage_z_to_xy(1)
    stage_finish(0, ga_ref)
    stage_finish(1, gb_ref)
    each(0, nt, lambda k: box_copy(k).wait_send())


def local(
    nf,
    nt,
    state,
    cotangent,
    block_peer,
    source_start,
    target_start,
    interp,
    sea_mask,
    w_first,
    w_down,
    w_up,
    w_out,
):
    nxy, nz = nf * 2, nt // 2
    na, nb = -(-55 // nxy), -(-48 // nxy)
    nblk = source_start.shape[-1]
    flat_state = state.reshape(CIN, 4 * LANES)
    flat_cot = cotangent.reshape(CIN, 4 * LANES)
    peer = block_peer.reshape(nblk)
    target = jnp.repeat(target_start.reshape(nt, 2).T.reshape(2 * nt), KC)[:, None]
    zero = jnp.zeros((BS, BS), BF)
    matrix = interp[0]
    pair = jnp.concatenate(
        [jnp.concatenate([matrix, zero], 1), jnp.concatenate([zero, matrix], 1)], 0
    )
    first = jnp.pad(
        w_first.reshape(3, 3, CH, CIN + KC), ((0, 0), (0, 0), (0, 0), (0, 12))
    )
    down = w_down.reshape(3, 3, 2 * CH, CH)
    up = w_up.reshape(3, 3, CH, 3 * CH)
    a1 = first.transpose(1, 2, 0, 3).reshape(3 * CH, 96)
    a2 = down.transpose(1, 2, 0, 3).reshape(6 * CH, 3 * CH)
    a3 = up.transpose(1, 2, 0, 3).reshape(3 * CH, 9 * CH)
    b2 = down[::-1, ::-1].transpose(1, 3, 0, 2).reshape(3 * CH, 6 * CH)
    b3 = up[::-1, ::-1].transpose(1, 3, 0, 2).reshape(9 * CH, 3 * CH)
    wo = w_out.reshape(CIN, CH)
    tables = [jnp.asarray(table, BF) for table in edge_tables()]
    operands = (
        flat_state,
        flat_cot,
        peer[None, :],
        peer[:, None],
        source_start.reshape(1, nblk),
        target,
        pair,
        sea_mask.reshape(4, LANES),
        a1,
        a2,
        a3,
        b2,
        b3,
        wo,
        wo.T,
        *tables,
    )
    dma = pltpu.SemaphoreType.DMA
    scratch = [
        pltpu.VMEM((nt, KC, LANES), F32),
        pltpu.VMEM((nt, KC, LANES), F32),
        pltpu.VMEM((N_EX, 2, LANES, LANES), BF),
        pltpu.VMEM((N_EX, 2, LANES, LANES), BF),
        pltpu.VMEM((N_EX, 16, LANES), BF),
        pltpu.VMEM((N_EX, 6, 16, LANES), BF),
        pltpu.VMEM((96, 5 * LANES), BF),
        pltpu.VMEM((3 * CH, 3 * LANES), BF),
        pltpu.VMEM((9 * CH, 5 * LANES), BF),
        pltpu.VMEM((3 * CH, 5 * LANES), BF),
        pltpu.VMEM((6 * CH, 3 * LANES), BF),
    ]
    for n in (na, nb):
        scratch += [
            pltpu.VMEM((nxy * n * 16, LANES), BF),
            pltpu.VMEM((nxy, n * 16, LANES), BF),
            pltpu.VMEM((n * 16, LANES), BF),
            pltpu.VMEM((n, nz, 16, LANES), BF),
            pltpu.VMEM((n * 16, LANES), BF),
            pltpu.VMEM((nxy * n * 16, LANES), BF),
        ]
    scratch += [
        dma((nt,)),
        dma((nt,)),
        dma((N_EX, 8)),
        dma((N_EX, 8)),
        dma((2, nxy)),
        dma((2, nxy)),
        dma((na + nb,)),
        dma((na + nb, nz)),
        dma((na + nb, nz)),
        dma((na + nb,)),
        dma((2, nxy)),
        dma((2, nxy)),
    ]
    vmem = pl.BlockSpec(memory_space=pltpu.VMEM)
    predicted, sums_a, sums_b = pl.pallas_call(
        functools.partial(kernel, nf, nt, na, nb),
        out_shape=(
            jax.ShapeDtypeStruct((CIN, 4 * LANES), BF),
            jax.ShapeDtypeStruct((nxy * na * 16, LANES), F32),
            jax.ShapeDtypeStruct((nxy * nb * 16, LANES), F32),
        ),
        in_specs=[vmem] * len(operands),
        out_specs=(vmem, vmem, vmem),
        scratch_shapes=scratch,
        compiler_params=pltpu.CompilerParams(
            collective_id=0, has_side_effects=True, vmem_limit_bytes=40 * 2**20
        ),
    )(*operands)

    grad_up = jnp.concatenate(
        [sums_a[192 * i : 192 * i + 192] for i in range(4)]
        + [jnp.concatenate([sums_a[768:864, 0:64], sums_a[768:864, 64:128]], 0)],
        axis=1,
    )
    grad_down = jnp.concatenate(
        [sums_b[0:384], jnp.concatenate([sums_b[384:576, 0:64], sums_b[384:576, 64:128]], 0)],
        axis=1,
    )
    grad_first = sums_b[576:768, 0:96].reshape(3, CH, 3, 32)[..., : CIN + KC]
    return (
        predicted.reshape(1, CIN, 4, LANES),
        grad_first.transpose(2, 0, 1, 3).reshape(1, 9, -1),
        grad_down.reshape(3, 2 * CH, 3, CH).transpose(2, 0, 1, 3).reshape(1, 9, -1),
        grad_up.reshape(3, CH, 3, 3 * CH).transpose(2, 0, 1, 3).reshape(1, 9, -1),
        sums_a[864:880, 0:64].reshape(1, -1),
    )


def solution(mesh):
    return jax.shard_map(
        functools.partial(local, mesh.shape["face"], mesh.shape["tile"]),
        mesh=mesh,
        in_specs=(
            P("half", None, "face", "tile"),
            P("half", None, "face", "tile"),
            P("half", "face", "tile", None, None),
            P("half", "face", "tile", None),
            P("half", "face", "tile", None, None),
            P("half", None, None),
            P("half", "face", "tile"),
            P("half", None, None),
            P("half", None, None),
            P("half", None, None),
            P("half", None),
        ),
        out_specs=(
            P("half", None, "face", "tile"),
            P("half", None, None),
            P("half", None, None),
            P("half", None, None),
            P("half", None),
        ),
        check_vma=False,
    )
```

```python
import functools
import math

import jax
import jax.numpy as jnp
import numpy as np
from jax import lax
from jax.experimental import pallas as pl
from jax.experimental.pallas import tpu as pltpu
from jax.sharding import PartitionSpec as P

CH = 64
CIN = 16
KC = 4
BS = 64
LANES = 128
GELU_C = math.sqrt(2.0 / math.pi)
BF = jnp.bfloat16
F32 = jnp.float32
MESH = pl.DeviceIdType.MESH
DIRS = [(-1, 0), (1, 0), (0, -1), (0, 1), (-1, -1), (-1, 1), (1, -1), (1, 1)]
OPP = [DIRS.index((-a, -b)) for a, b in DIRS]
N_EX = 5
EX_CH = (32, 128, 128, 64, 128)


def gelu_pair(pre):
    inner = jnp.tanh(GELU_C * (pre + 0.044715 * pre * pre * pre))
    value = 0.5 * pre * (1.0 + inner)
    slope = 0.5 * (1.0 + inner) + 0.5 * pre * (1.0 - inner * inner) * GELU_C * (
        1.0 + 3.0 * 0.044715 * pre * pre
    )
    return value, slope


def roll(x, shift):
    return pltpu.roll(x, shift % LANES, axis=1)


def lanes_of(rows):
    return lax.broadcasted_iota(jnp.int32, (rows, LANES), 1)


def barrel(x, amount, right):
    for bit in range(7):
        step = 1 << bit
        moved = roll(x, step if right else LANES - step)
        x = jnp.where((amount & step) != 0, moved, x)
    return x


def pair_sum(x):
    even = (lanes_of(x.shape[0]) & 1) == 0
    return x + jnp.where(even, roll(x, -1), roll(x, 1))


def edge_tables():
    pick_fine = np.zeros((16, 4 * LANES), np.float32)
    pick_coarse = np.zeros((16, 2 * LANES), np.float32)
    for base, lane in ((0, LANES - 1), (8, 0)):
        for j, row in enumerate((3, 0, 1, 2, 3, 0)):
            pick_fine[base + j, row * LANES + lane] = 1
            pick_coarse[base + j, (row // 2) * LANES + lane] = 1
    place_fine = np.zeros((3, 16, LANES), np.float32)
    place_coarse = np.zeros((3, 16, LANES), np.float32)
    for a in range(3):
        for base, start in ((0, 0), (8, 64)):
            for r in range(4):
                place_fine[a, base + r + a, start + r] = 1
            for r in range(2):
                place_coarse[a, base + (0, 1, 3, 5)[r + a], start + r] = 1
    return pick_fine, pick_coarse, place_fine, place_coarse


def weight_tables():
    up = np.zeros((576, 288), np.float32)
    down = np.zeros((1152, 576), np.float32)
    for b in range(3):
        for a in range(3):
            k = 3 * (2 - a) + 2 - b
            for o in range(CH):
                up[(b * 3 + a) * CH + o, 8 * (o // 2) + k if k < 8 else 256 + o // 2] = 1
            for o in range(2 * CH):
                down[(b * 3 + a) * 2 * CH + o, 8 * (o // 2) + k if k < 8 else 512 + o // 2] = 1
    wide = CIN + KC
    lane = np.arange(CH * wide)
    mask = (lane[None, :] // wide == np.arange(CH)[:, None]).astype(np.float32)
    fold = (lane[:, None] % wide == np.arange(32)[None, :]).astype(np.float32)
    return up, down, mask, fold


def conv_rows(weight, x_ref, outs, rows, step):
    z = jnp.dot(weight, x_ref[...], preferred_element_type=F32)
    lane = lanes_of(outs)
    halo_left = z[:outs, rows * LANES :]
    halo_right = z[2 * outs :, rows * LANES :]
    result = []
    for r in range(rows):
        at = slice(r * LANES, (r + 1) * LANES)
        left = jnp.where(lane < step, halo_left[:, r : r + 1], roll(z[:outs, at], step))
        right = jnp.where(
            lane >= LANES - step, halo_right[:, 64 + r : 65 + r], roll(z[2 * outs :, at], -step)
        )
        result.append(z[outs : 2 * outs, at] + left + right)
    return result


def weight_grad(delta_rows, x_ref, step):
    outs = delta_rows[0].shape[0]
    lane = lanes_of(outs)
    keep = (lane & (step - 1)) == 0
    zero = jnp.zeros((outs, LANES), F32)
    first, middle, last = [], [], []
    halo_left, halo_right = zero, zero
    for r, delta in enumerate(delta_rows):
        first.append(jnp.where(keep & (lane < LANES - step), roll(delta, -step), 0.0))
        middle.append(jnp.where(keep, delta, 0.0))
        last.append(jnp.where(keep & (lane >= step), roll(delta, step), 0.0))
        halo_left = jnp.where(lane == r, delta[:, 0:1], halo_left)
        halo_right = jnp.where(lane == 64 + r, delta[:, LANES - 1 : LANES], halo_right)
    parts = [first + [halo_left], middle + [zero], last + [halo_right]]
    stacked = jnp.concatenate(
        [jnp.concatenate(part, axis=1).astype(BF) for part in parts], axis=0
    )
    return lax.dot_general(
        stacked, x_ref[...], (((1,), (1,)), ((), ())), preferred_element_type=F32
    )


def kernel(
    nf,
    nt,
    na,
    nb,
    nc,
    state_hbm,
    cot_hbm,
    peer_hbm,
    src_hbm,
    tgt_hbm,
    interp_hbm,
    sea_hbm,
    w1_hbm,
    w2_hbm,
    w3_hbm,
    wo_hbm,
    up_hbm,
    down_hbm,
    mask_hbm,
    fold_hbm,
    pickf_hbm,
    pickc_hbm,
    placef_hbm,
    placec_hbm,
    pred_ref,
    ga_ref,
    gb_ref,
    gc_ref,
    state_ref,
    cot_ref,
    peer_ref,
    src_ref,
    tgt_ref,
    interp_ref,
    sea_ref,
    w1_ref,
    w2_ref,
    w3_ref,
    wo_ref,
    up_ref,
    down_ref,
    mask_ref,
    fold_ref,
    pickf_ref,
    pickc_ref,
    placef_ref,
    placec_ref,
    load_sem,
    s2,
    s3,
    a1,
    a2,
    a3,
    b2,
    b3,
    outbox,
    inbox,
    row_send,
    row_recv,
    edge_send,
    edge_recv,
    x1,
    x2,
    x3,
    xd3,
    xd2,
    send_a,
    recv_a,
    part_a,
    zrecv_a,
    done_a,
    all_a,
    send_b,
    recv_b,
    part_b,
    zrecv_b,
    done_b,
    all_b,
    send_c,
    recv_c,
    part_c,
    zrecv_c,
    done_c,
    all_c,
    box_ssem,
    box_rsem,
    ex_ssem,
    ex_rsem,
    xy_ssem,
    xy_rsem,
    zs_ssem,
    zs_rsem,
    zg_ssem,
    zg_rsem,
    gx_ssem,
    gx_rsem,
    za_ssem,
    za_rsem,
):
    half = lax.axis_index("half")
    face = lax.axis_index("face")
    tile = lax.axis_index("tile")
    nz = nt // 2
    nxy = nf * 2
    y_hi = tile // nz
    z = tile % nz
    me_xy = face * 2 + y_hi

    def xy_peer(k):
        other = (me_xy + k) % nxy
        return other, {"face": other // 2, "tile": (other % 2) * nz + z}

    def z_peer(k):
        other = (z + k) % nz
        return other, {"tile": y_hi * nz + other}

    def box_peer(k):
        other = (tile + k) % nt
        return other, {"half": 1 - half, "tile": other}

    def neighbour(d):
        df, dt = DIRS[d]
        ok = (face + df >= 0) & (face + df < nf) & (tile + dt >= 0) & (tile + dt < nt)
        return ok, {"face": face + df, "tile": tile + dt}

    loads = [
        pltpu.make_async_copy(src, dst, load_sem.at[i])
        for i, (src, dst) in enumerate(
            (
                (state_hbm, state_ref),
                (peer_hbm, peer_ref),
                (src_hbm, src_ref),
                (w3_hbm, w3_ref),
                (up_hbm, up_ref),
                (w2_hbm, w2_ref),
                (down_hbm, down_ref),
                (w1_hbm, w1_ref),
                (mask_hbm, mask_ref),
                (fold_hbm, fold_ref),
                (wo_hbm, wo_ref),
                (tgt_hbm, tgt_ref),
                (interp_hbm, interp_ref),
                (sea_hbm, sea_ref),
                (cot_hbm, cot_ref),
                (pickf_hbm, pickf_ref),
                (pickc_hbm, pickc_ref),
                (placef_hbm, placef_ref),
                (placec_hbm, placec_ref),
            )
        )
    ]
    for load in loads:
        load.start()

    row_recv[...] = jnp.zeros_like(row_recv)
    edge_recv[...] = jnp.zeros_like(edge_recv)
    edge_send[...] = jnp.zeros_like(edge_send)

    barrier = pltpu.get_barrier_semaphore()

    def greet(peer, count):
        def body(k, carry):
            pl.semaphore_signal(barrier, inc=1, device_id=peer(k)[1], device_id_type=MESH)
            return carry

        lax.fori_loop(count[0], count[1], body, 0)

    greet(box_peer, (0, nt))
    greet(xy_peer, (1, nxy))
    greet(z_peer, (1, nz))
    expected = nt + nxy - 1 + nz - 1
    for d in range(8):
        ok, device = neighbour(d)
        expected = expected + ok.astype(jnp.int32)

        @pl.when(ok)
        def _(device=device):
            pl.semaphore_signal(barrier, inc=1, device_id=device, device_id_type=MESH)

    rows = 2 * nt * KC
    nblk = src_ref.shape[1]
    for load in loads[:3]:
        load.wait()
    state3 = state_ref[...].astype(F32)
    state_rows = [state3[:, q, :] for q in range(4)]
    peer_col = jnp.broadcast_to(peer_ref[...], (nblk, nblk))
    diagonal = lax.broadcasted_iota(jnp.int32, (nblk, nblk), 0) == lax.broadcasted_iota(
        jnp.int32, (nblk, nblk), 1
    )
    peer_row = jnp.sum(jnp.where(diagonal, peer_col, 0), axis=0, keepdims=True)
    same = peer_col == peer_row
    earlier = lax.broadcasted_iota(jnp.int32, (nblk, nblk), 0) < lax.broadcasted_iota(
        jnp.int32, (nblk, nblk), 1
    )
    rank = jnp.sum(jnp.where(same & earlier, 1.0, 0.0), axis=0, keepdims=True)
    row_id = lax.broadcasted_iota(jnp.int32, (rows, nblk), 0)
    slot = (row_id // (nt * KC)).astype(F32)
    match = ((row_id // KC) % nt == peer_row) & (slot == rank)
    used = jnp.sum(jnp.where(match, 1.0, 0.0), axis=1, keepdims=True)
    start = jnp.sum(
        jnp.where(match, src_ref[...].astype(F32), 0.0), axis=1, keepdims=True
    ).astype(jnp.int32)
    start = jnp.broadcast_to(start, (rows, LANES))
    lane = lanes_of(rows)
    sub8 = lax.broadcasted_iota(jnp.int32, (8, LANES), 0)
    shift = start & (LANES - 1)
    from_tile = (start >> 7) + (lane < shift).astype(jnp.int32)
    window = jnp.zeros((rows, LANES), F32)
    for q in range(4):
        head = state_rows[q][0:8]
        head = jnp.where(sub8 < KC, head, pltpu.roll(head, 4, axis=0))
        window = jnp.where(
            from_tile == q, jnp.concatenate([head] * (rows // 8), axis=0), window
        )
    window = barrel(window, shift, False)
    window = jnp.where((lane < BS) & (used > 0.0), window, 0.0)
    packed = window[: rows // 2] + roll(window[rows // 2 :], BS)
    for p in range(nt):
        outbox[p] = packed[p * KC : (p + 1) * KC]

    pl.semaphore_wait(barrier, expected)

    def box_copy(k):
        other, device = box_peer(k)
        return pltpu.make_async_remote_copy(
            src_ref=outbox.at[other],
            dst_ref=inbox.at[tile],
            send_sem=box_ssem.at[k],
            recv_sem=box_rsem.at[tile],
            device_id=device,
            device_id_type=MESH,
        )

    def box_arrival(k):
        other, device = box_peer(k)
        return pltpu.make_async_remote_copy(
            src_ref=outbox.at[other],
            dst_ref=inbox.at[other],
            send_sem=box_ssem.at[k],
            recv_sem=box_rsem.at[other],
            device_id=device,
            device_id_type=MESH,
        )

    def each(low, high, act):
        def body(k, carry):
            act(k)
            return carry

        lax.fori_loop(low, high, body, 0)

    each(0, nt, lambda k: box_copy(k).start())

    for load in loads[3:]:
        load.wait()
    for j in range(CH // 2):
        part = w3_ref[:, 384 * j : 384 * j + 384].astype(F32)
        s3[8 * j : 8 * j + 8] = part[0:8]
        s3[256 + j : 257 + j] = part[8:9]
    for j in range(CH):
        part = w2_ref[:, 128 * j : 128 * j + 128].astype(F32)
        s2[8 * j : 8 * j + 8] = part[0:8]
        s2[512 + j : 513 + j] = part[8:9]
    taps = jnp.dot(up_ref[...], s3[...].astype(BF), preferred_element_type=F32)
    odd = (lax.broadcasted_iota(jnp.int32, (576, 192), 0) & 1) == 1
    taps = jnp.where(odd, taps[:, 192:384], taps[:, 0:192])
    for b in range(3):
        b3[192 * b : 192 * b + 192] = taps[192 * b : 192 * b + 192].T.astype(BF)
        for a in range(3):
            at = ((2 - b) * 3 + 2 - a) * CH
            a3[CH * b : CH * b + CH, 192 * a : 192 * a + 192] = taps[at : at + CH].astype(BF)
    taps = jnp.dot(down_ref[...], s2[...].astype(BF), preferred_element_type=F32)
    odd = (lax.broadcasted_iota(jnp.int32, (1152, LANES), 0) & 1) == 1
    taps = jnp.where(odd, roll(taps, CH), taps)
    for b in range(3):
        b2[CH * b : CH * b + CH] = taps[384 * b : 384 * b + 384].T[0:CH].astype(BF)
        for a in range(3):
            at = ((2 - b) * 3 + 2 - a) * 2 * CH
            a2[2 * CH * b : 2 * CH * b + 2 * CH, CH * a : CH * a + CH] = taps[
                at : at + 2 * CH, 0:CH
            ].astype(BF)
    flat_first = w1_ref[...].astype(F32)
    for k in range(9):
        spread = mask_ref[...].astype(F32) * flat_first[k : k + 1]
        a1[CH * (k % 3) : CH * (k % 3) + CH, 32 * (k // 3) : 32 * (k // 3) + 32] = jnp.dot(
            spread.astype(BF), fold_ref[...], preferred_element_type=F32
        ).astype(BF)
    wo32 = jnp.zeros((16, LANES), F32)
    sub16 = lax.broadcasted_iota(jnp.int32, (16, LANES), 0)
    for j in range(CIN // 2):
        part = jnp.broadcast_to(
            wo_ref[0:1, LANES * j : LANES * j + LANES].astype(F32), (16, LANES)
        )
        wo32 = jnp.where(sub16 == 2 * j, part, wo32)
        wo32 = jnp.where(sub16 == 2 * j + 1, roll(part, CH), wo32)
    wo = wo32[:, 0:CH].astype(BF)
    wot = wo32.T[0:CH].astype(BF)
    zero64 = jnp.zeros((BS, BS), F32)
    one = interp_ref[...].astype(F32)
    matrix = jnp.concatenate(
        [jnp.concatenate([one, zero64], axis=1), jnp.concatenate([zero64, one], axis=1)], axis=0
    ).astype(BF)
    cot3 = cot_ref[...].astype(F32)
    cot = jnp.concatenate([cot3[:, q, :] for q in range(4)], axis=1).astype(BF)
    wanted = tgt_ref[...] & 511
    halves = jnp.concatenate([wanted >> 6, wanted & 63], axis=1).astype(F32).astype(BF)
    own_row = lax.broadcasted_iota(jnp.int32, (rows, nt), 0)
    own_peer = lax.broadcasted_iota(jnp.int32, (rows, nt), 1)
    copies = jnp.where((own_row // KC) % nt == own_peer, 1.0, 0.0).astype(BF)
    spots = jnp.dot(copies, halves, preferred_element_type=F32)
    first_slot = lax.broadcasted_iota(jnp.int32, (rows, 1), 0) < nt * KC
    target = jnp.where(
        first_slot, spots[:, 0:1] * 64.0 + spots[:, 2:3], spots[:, 1:2] * 64.0 + spots[:, 3:4]
    ).astype(jnp.int32)

    def ex_copy(e, d, arrival):
        ok, device = neighbour(d)
        at = d if arrival else OPP[d]
        if d < 2:
            src = row_send.at[e, d, 0 : EX_CH[e]]
            dst = row_recv.at[e, at, 0 : EX_CH[e]]
        else:
            src = edge_send.at[e]
            dst = edge_recv.at[e, at - 2]
        return ok, pltpu.make_async_remote_copy(
            src_ref=src,
            dst_ref=dst,
            send_sem=ex_ssem.at[e, d],
            recv_sem=ex_rsem.at[e, at],
            device_id=device,
            device_id_type=MESH,
        )

    def ex_start(e):
        for d in range(8):
            ok, copy = ex_copy(e, d, False)
            pl.when(ok)(copy.start)

    def ex_wait(e):
        for d in range(8):
            ok, copy = ex_copy(e, d, True)

            @pl.when(ok)
            def _(copy=copy):
                copy.wait_recv()
                copy.wait_send()

    def pick(table_ref, field):
        return lax.dot_general(
            table_ref[...], field, (((1,), (1,)), ((), ())), preferred_element_type=F32
        ).astype(BF)

    takes = {
        2: (sub16 >= 1) & (sub16 <= 4),
        3: (sub16 >= 9) & (sub16 <= 12),
        4: sub16 == 0,
        5: sub16 == 8,
        6: sub16 == 5,
        7: sub16 == 13,
    }

    def halo_columns(e):
        held = jnp.zeros((16, LANES), F32)
        for d in range(2, 8):
            held = jnp.where(takes[d], edge_recv[e, d - 2].astype(F32), held)
        return held.T

    def place(columns, table_ref, a):
        return jnp.dot(
            columns.astype(BF), table_ref[a], preferred_element_type=F32
        ).astype(BF)

    def fill_centre(x_ref, chans, offset, total, field_rows):
        count = len(field_rows)
        for a in range(3):
            for r in range(count):
                if 1 <= r + a <= count:
                    x_ref[
                        a * total + offset : a * total + offset + chans,
                        r * LANES : (r + 1) * LANES,
                    ] = field_rows[r + a - 1]

    def fill_halo(x_ref, chans, offset, total, count, above, below, columns, table_ref):
        x_ref[offset : offset + chans, 0:LANES] = above
        x_ref[
            2 * total + offset : 2 * total + offset + chans, (count - 1) * LANES : count * LANES
        ] = below
        for a in range(3):
            x_ref[
                a * total + offset : a * total + offset + chans, count * LANES :
            ] = place(columns, table_ref, a)

    groups = (
        (na, send_a, recv_a, part_a, zrecv_a, done_a, all_a, 0),
        (nb, send_b, recv_b, part_b, zrecv_b, done_b, all_b, 2),
        (nc, send_c, recv_c, part_c, zrecv_c, done_c, all_c, 0),
    )

    def xy_copy(g, k, arrival):
        other, device = xy_peer(k)
        send, recv, m = groups[g][1], groups[g][2], 16 * groups[g][0]
        at = other if arrival else me_xy
        return pltpu.make_async_remote_copy(
            src_ref=send.at[pl.ds(pl.multiple_of(other * m, 16), m)],
            dst_ref=recv.at[at],
            send_sem=xy_ssem.at[g, k],
            recv_sem=xy_rsem.at[g, at],
            device_id=device,
            device_id_type=MESH,
        )

    def xy_start(g):
        each(1, nxy, lambda k: xy_copy(g, k, False).start())

    def z_owner(g, q):
        return (4 * q + groups[g][7]) % nz

    def zs_copy(g, q, source):
        n, send, recv, part, zrecv, done, full, first = groups[g]
        base = 0 if g == 0 else na
        return pltpu.make_async_remote_copy(
            src_ref=part.at[16 * q : 16 * q + 16],
            dst_ref=zrecv.at[q, source],
            send_sem=zs_ssem.at[base + q],
            recv_sem=zs_rsem.at[base + q, source],
            device_id={"tile": y_hi * nz + z_owner(g, q)},
            device_id_type=MESH,
        )

    def zg_copy(g, q, k):
        n, send, recv, part, zrecv, done, full, first = groups[g]
        base = 0 if g == 0 else na
        return pltpu.make_async_remote_copy(
            src_ref=done.at[16 * q : 16 * q + 16],
            dst_ref=done.at[16 * q : 16 * q + 16],
            send_sem=zg_ssem.at[base + q, k],
            recv_sem=zg_rsem.at[base + q],
            device_id=z_peer(k)[1],
            device_id_type=MESH,
        )

    def gx_copy(g, k, arrival):
        other, device = xy_peer(k)
        n, send, recv, part, zrecv, done, full, first = groups[g]
        m = 16 * n
        at = other if arrival else me_xy
        return pltpu.make_async_remote_copy(
            src_ref=done,
            dst_ref=full.at[pl.ds(pl.multiple_of(at * m, 16), m)],
            send_sem=gx_ssem.at[g, k],
            recv_sem=gx_rsem.at[g, at],
            device_id=device,
            device_id_type=MESH,
        )

    def zall_copy(k, arrival):
        other, device = z_peer(k)
        return pltpu.make_async_remote_copy(
            src_ref=part_c,
            dst_ref=zrecv_c.at[other if arrival else z],
            send_sem=za_ssem.at[k],
            recv_sem=za_rsem.at[other if arrival else z],
            device_id=device,
            device_id_type=MESH,
        )

    def stage_all_z():
        each(1, nz, lambda k: zall_copy(k, True).wait_recv())
        zrecv_c[z] = part_c[...]
        total = zrecv_c[0].astype(F32)
        for j in range(1, nz):
            total = total + zrecv_c[j].astype(F32)
        done_c[...] = total.astype(BF)
        each(1, nxy, lambda k: gx_copy(2, k, False).start())

    def stage_xy_to_z(g):
        n, send, recv, part, zrecv, done, full, first = groups[g]
        m = 16 * n
        total = send[pl.ds(pl.multiple_of(me_xy * m, 16), m), :].astype(F32)
        each(1, nxy, lambda k: xy_copy(g, k, True).wait_recv())
        recv[me_xy] = jnp.zeros((m, LANES), BF)
        for j in range(nxy):
            total = total + recv[j].astype(F32)
        part[...] = total.astype(BF)
        if g == 2:
            each(1, nz, lambda k: zall_copy(k, False).start())
            return
        for q in range(n):

            @pl.when(z != z_owner(g, q))
            def _(q=q):
                zs_copy(g, q, z).start()

    def stage_z_reduce(g):
        n, send, recv, part, zrecv, done, full, first = groups[g]
        for q in range(n):

            @pl.when(z == z_owner(g, q))
            def _(q=q):
                each(1, nz, lambda k: zs_copy(g, q, z_peer(k)[0]).wait_recv())
                zrecv[q, z] = part[16 * q : 16 * q + 16]
                total = jnp.zeros((16, LANES), F32)
                for j in range(nz):
                    total = total + zrecv[q, j].astype(F32)
                done[16 * q : 16 * q + 16] = total.astype(BF)
                each(1, nz, lambda k: zg_copy(g, q, k).start())

    def stage_z_to_xy(g):
        n, send, recv, part, zrecv, done, full, first = groups[g]
        for q in range(n):

            @pl.when(z != z_owner(g, q))
            def _(q=q):
                zg_copy(g, q, 1).wait_recv()

        each(1, nxy, lambda k: gx_copy(g, k, False).start())

    def stage_finish(g, out_ref):
        n, send, recv, part, zrecv, done, full, first = groups[g]
        m = 16 * n
        each(1, nxy, lambda k: gx_copy(g, k, True).wait_recv())
        full[pl.ds(pl.multiple_of(me_xy * m, 16), m), :] = done[...]
        scale = 1.0 / math.sqrt(nf * 4 * nt * LANES)
        out_ref[...] = full[...].astype(F32) * scale
        each(1, nxy, lambda k: xy_copy(g, k, False).wait_send())
        each(1, nxy, lambda k: gx_copy(g, k, False).wait_send())
        if g == 2:
            each(1, nz, lambda k: zall_copy(k, False).wait_send())
            return
        for q in range(n):

            @pl.when(z != z_owner(g, q))
            def _(q=q):
                zs_copy(g, q, z).wait_send()

            @pl.when(z == z_owner(g, q))
            def _(q=q):
                each(1, nz, lambda k: zg_copy(g, q, k).wait_send())

    target = jnp.broadcast_to(target, (rows, LANES))
    shift_in = target & (LANES - 1)
    to_tile = (target >> 7) + (lane < shift_in).astype(jnp.int32)
    each(0, nt, lambda k: box_arrival(k).wait_recv())
    arrived = jnp.concatenate([inbox[p] for p in range(nt)], axis=0)
    moved = jnp.dot(arrived.astype(BF), matrix, preferred_element_type=F32)
    lane_half = lanes_of(rows // 2)
    moved = jnp.concatenate(
        [
            jnp.where(lane_half < BS, moved, 0.0),
            roll(jnp.where(lane_half >= BS, moved, 0.0), BS),
        ],
        axis=0,
    )
    moved = barrel(moved, shift_in, True)
    lifted = []
    for q in range(4):
        chosen = jnp.where(to_tile == q, moved, 0.0)
        total = chosen[0:8]
        for i in range(1, rows // 8):
            total = total + chosen[8 * i : 8 * i + 8]
        total = total + pltpu.roll(total, 4, axis=0)
        total = total * sea_ref[q : q + 1, :].astype(F32)
        forcing = jnp.concatenate(
            [jnp.where(sub8 < KC, total, 0.0), jnp.zeros((8, LANES), F32)], axis=0
        ).astype(BF)
        lifted.append(
            jnp.concatenate([state_rows[q].astype(BF), forcing], axis=0)
        )

    row_send[0, 0, 0:32] = lifted[0]
    row_send[0, 1, 0:32] = lifted[3]
    edge_send[0, :, 0:32] = pick(pickf_ref, jnp.concatenate(lifted, axis=1))
    ex_start(0)
    fill_centre(x1, 32, 0, 32, lifted)
    ex_wait(0)
    columns = halo_columns(0)[0:32]
    fill_halo(
        x1, 32, 0, 32, 4, row_recv[0, 0, 0:32], row_recv[0, 1, 0:32], columns, placef_ref
    )
    pre = conv_rows(a1[...], x1, CH, 4, 1)
    hidden_one, slope_one = [], []
    for r in range(4):
        value, slope = gelu_pair(pre[r])
        hidden_one.append(value.astype(BF))
        slope_one.append(slope)
    pooled = [
        (
            pair_sum(hidden_one[2 * r].astype(F32) + hidden_one[2 * r + 1].astype(F32)) * 0.25
        ).astype(BF)
        for r in range(2)
    ]

    for at, fine, coarse in ((0, 0, 0), (1, 3, 1)):
        row_send[1, at, 0:CH] = hidden_one[fine]
        row_send[1, at, CH : 2 * CH] = pooled[coarse]
    edge_send[1] = jnp.concatenate(
        [
            pick(pickf_ref, jnp.concatenate(hidden_one, axis=1)),
            pick(pickc_ref, jnp.concatenate(pooled, axis=1)),
        ],
        axis=1,
    )
    ex_start(1)
    fill_centre(x3, CH, 0, 3 * CH, hidden_one)
    fill_centre(x2, CH, 0, CH, pooled)
    ex_wait(1)
    columns = halo_columns(1)
    fill_halo(
        x2,
        CH,
        0,
        CH,
        2,
        row_recv[1, 0, CH : 2 * CH],
        row_recv[1, 1, CH : 2 * CH],
        columns[CH : 2 * CH],
        placec_ref,
    )
    pre = conv_rows(a2[...], x2, 2 * CH, 2, 2)
    hidden_two, slope_two = [], []
    for r in range(2):
        value, slope = gelu_pair(pre[r])
        hidden_two.append(value.astype(BF))
        slope_two.append(slope)

    row_send[2, 0] = hidden_two[0]
    row_send[2, 1] = hidden_two[1]
    edge_send[2] = pick(pickc_ref, jnp.concatenate(hidden_two, axis=1))
    ex_start(2)
    fill_halo(
        x3, CH, 0, 3 * CH, 4, row_recv[1, 0, 0:CH], row_recv[1, 1, 0:CH], columns[0:CH], placef_ref
    )
    fill_centre(x3, 2 * CH, CH, 3 * CH, [hidden_two[r // 2] for r in range(4)])
    back_three = jnp.dot(wot, cot, preferred_element_type=F32)
    ex_wait(2)
    columns = halo_columns(2)
    fill_halo(
        x3, 2 * CH, CH, 3 * CH, 4, row_recv[2, 0], row_recv[2, 1], columns, placef_ref
    )
    pre = conv_rows(a3[...], x3, CH, 4, 1)
    hidden_three, delta_three = [], []
    for r in range(4):
        value, slope = gelu_pair(pre[r])
        hidden_three.append(value.astype(BF))
        delta_three.append(
            (back_three[:, r * LANES : (r + 1) * LANES] * slope).astype(BF)
        )

    row_send[3, 0, 0:CH] = delta_three[0]
    row_send[3, 1, 0:CH] = delta_three[3]
    edge_send[3, :, 0:CH] = pick(pickf_ref, jnp.concatenate(delta_three, axis=1))
    ex_start(3)
    fill_centre(xd3, CH, 0, CH, delta_three)
    flat_three = jnp.concatenate(hidden_three, axis=1)
    pred_ref[...] = (
        jnp.concatenate(state_rows, axis=1)
        + jnp.dot(wo, flat_three, preferred_element_type=F32)
    ).astype(BF)
    grad_out = lax.dot_general(
        cot, flat_three, (((1,), (1,)), ((), ())), preferred_element_type=F32
    )
    grad_up = weight_grad([d.astype(F32) for d in delta_three], x3, 1)
    for block in range(4):
        send_a[192 * block : 192 * block + 192] = grad_up[
            :, block * LANES : (block + 1) * LANES
        ].astype(BF)
    send_a[768:864] = jnp.concatenate([grad_up[0:96, 512:576], grad_up[96:192, 512:576]], axis=1).astype(BF)
    send_a[864:880] = jnp.concatenate([grad_out, jnp.zeros((16, 64), F32)], axis=1).astype(BF)
    if 16 * na * nxy > 880:
        send_a[880:] = jnp.zeros((16 * na * nxy - 880, LANES), BF)
    xy_start(0)
    ex_wait(3)
    columns = halo_columns(3)[0:CH]
    fill_halo(
        xd3, CH, 0, CH, 4, row_recv[3, 0, 0:CH], row_recv[3, 1, 0:CH], columns, placef_ref
    )
    join = conv_rows(b3[...], xd3, 3 * CH, 4, 1)
    delta_two = [
        (pair_sum(join[2 * r][CH:] + join[2 * r + 1][CH:]) * slope_two[r]).astype(BF)
        for r in range(2)
    ]

    row_send[4, 0] = delta_two[0]
    row_send[4, 1] = delta_two[1]
    edge_send[4] = pick(pickc_ref, jnp.concatenate(delta_two, axis=1))
    ex_start(4)
    fill_centre(xd2, 2 * CH, 0, 2 * CH, delta_two)
    grad_down = weight_grad([d.astype(F32) for d in delta_two], x2, 2)
    send_b[0:384] = grad_down[:, 0:LANES].astype(BF)
    send_b[384:576] = jnp.concatenate([grad_down[0:192, 128:192], grad_down[192:384, 128:192]], axis=1).astype(BF)
    if 16 * nb * nxy > 576:
        send_b[576:] = jnp.zeros((16 * nb * nxy - 576, LANES), BF)
    xy_start(1)
    stage_xy_to_z(0)
    ex_wait(4)
    columns = halo_columns(4)
    fill_halo(
        xd2, 2 * CH, 0, 2 * CH, 2, row_recv[4, 0], row_recv[4, 1], columns, placec_ref
    )
    d_pool = conv_rows(b2[...], xd2, CH, 2, 2)
    delta_one = [
        ((join[r][0:CH] + 0.25 * d_pool[r // 2]) * slope_one[r]).astype(BF).astype(F32)
        for r in range(4)
    ]
    grad_first = weight_grad(delta_one, x1, 1)
    send_c[0:192] = jnp.concatenate([grad_first, jnp.zeros((192, 32), F32)], axis=1).astype(BF)
    if 16 * nc * nxy > 192:
        send_c[192:] = jnp.zeros((16 * nc * nxy - 192, LANES), BF)
    xy_start(2)
    stage_xy_to_z(1)
    stage_z_reduce(0)
    stage_xy_to_z(2)
    stage_z_reduce(1)
    stage_z_to_xy(0)
    stage_all_z()
    stage_z_to_xy(1)
    stage_finish(0, ga_ref)
    stage_finish(2, gc_ref)
    stage_finish(1, gb_ref)
    each(0, nt, lambda k: box_copy(k).wait_send())


def local(
    nf,
    nt,
    state,
    cotangent,
    block_peer,
    source_start,
    target_start,
    interp,
    sea_mask,
    w_first,
    w_down,
    w_up,
    w_out,
):
    nxy, nz = nf * 2, nt // 2
    na, nb, nc = -(-55 // nxy), -(-36 // nxy), -(-12 // nxy)
    nblk = source_start.shape[-1]
    tables = [jnp.asarray(table, BF) for table in weight_tables() + edge_tables()]
    operands = (
        state[0],
        cotangent[0],
        block_peer.reshape(nblk, 1),
        source_start.reshape(1, nblk),
        target_start.reshape(nt, 2),
        interp[0],
        sea_mask[0],
        w_first[0],
        w_down[0],
        w_up[0],
        w_out,
        *tables,
    )
    dma = pltpu.SemaphoreType.DMA
    scratch = [pltpu.VMEM(op.shape, op.dtype) for op in operands]
    scratch += [
        dma((len(operands),)),
        pltpu.VMEM((576, LANES), F32),
        pltpu.VMEM((288, 384), F32),
        pltpu.VMEM((3 * CH, 96), BF),
        pltpu.VMEM((6 * CH, 3 * CH), BF),
        pltpu.VMEM((3 * CH, 9 * CH), BF),
        pltpu.VMEM((3 * CH, 6 * CH), BF),
        pltpu.VMEM((9 * CH, 3 * CH), BF),
        pltpu.VMEM((nt, KC, LANES), F32),
        pltpu.VMEM((nt, KC, LANES), F32),
        pltpu.VMEM((N_EX, 2, LANES, LANES), BF),
        pltpu.VMEM((N_EX, 2, LANES, LANES), BF),
        pltpu.VMEM((N_EX, 16, LANES), BF),
        pltpu.VMEM((N_EX, 6, 16, LANES), BF),
        pltpu.VMEM((96, 5 * LANES), BF),
        pltpu.VMEM((3 * CH, 3 * LANES), BF),
        pltpu.VMEM((9 * CH, 5 * LANES), BF),
        pltpu.VMEM((3 * CH, 5 * LANES), BF),
        pltpu.VMEM((6 * CH, 3 * LANES), BF),
    ]
    for n in (na, nb, nc):
        scratch += [
            pltpu.VMEM((nxy * n * 16, LANES), BF),
            pltpu.VMEM((nxy, n * 16, LANES), BF),
            pltpu.VMEM((n * 16, LANES), BF),
            pltpu.VMEM((nz, n * 16, LANES) if n == nc else (n, nz, 16, LANES), BF),
            pltpu.VMEM((n * 16, LANES), BF),
            pltpu.VMEM((nxy * n * 16, LANES), BF),
        ]
    scratch += [
        dma((nt,)),
        dma((nt,)),
        dma((N_EX, 8)),
        dma((N_EX, 8)),
        dma((3, nxy)),
        dma((3, nxy)),
        dma((na + nb,)),
        dma((na + nb, nz)),
        dma((na + nb, nz)),
        dma((na + nb,)),
        dma((3, nxy)),
        dma((3, nxy)),
        dma((nz,)),
        dma((nz,)),
    ]
    vmem = pl.BlockSpec(memory_space=pltpu.VMEM)
    predicted, sums_a, sums_b, sums_c = pl.pallas_call(
        functools.partial(kernel, nf, nt, na, nb, nc),
        out_shape=(
            jax.ShapeDtypeStruct((CIN, 4 * LANES), BF),
            jax.ShapeDtypeStruct((nxy * na * 16, LANES), F32),
            jax.ShapeDtypeStruct((nxy * nb * 16, LANES), F32),
            jax.ShapeDtypeStruct((nxy * nc * 16, LANES), F32),
        ),
        in_specs=[pl.BlockSpec(memory_space=pl.ANY)] * len(operands),
        out_specs=(vmem,) * 4,
        scratch_shapes=scratch,
        compiler_params=pltpu.CompilerParams(
            collective_id=0, has_side_effects=True, vmem_limit_bytes=40 * 2**20
        ),
    )(*operands)

    grad_up = jnp.concatenate(
        [sums_a[192 * i : 192 * i + 192] for i in range(4)]
        + [jnp.concatenate([sums_a[768:864, 0:64], sums_a[768:864, 64:128]], 0)],
        axis=1,
    )
    grad_down = jnp.concatenate(
        [sums_b[0:384], jnp.concatenate([sums_b[384:576, 0:64], sums_b[384:576, 64:128]], 0)],
        axis=1,
    )
    grad_first = sums_c[0:192, 0:96].reshape(3, CH, 3, 32)[..., : CIN + KC]
    return (
        predicted.reshape(1, CIN, 4, LANES),
        grad_first.transpose(2, 0, 1, 3).reshape(1, 9, -1),
        grad_down.reshape(3, 2 * CH, 3, CH).transpose(2, 0, 1, 3).reshape(1, 9, -1),
        grad_up.reshape(3, CH, 3, 3 * CH).transpose(2, 0, 1, 3).reshape(1, 9, -1),
        sums_a[864:880, 0:64].reshape(1, -1),
    )


def solution(mesh):
    return jax.shard_map(
        functools.partial(local, mesh.shape["face"], mesh.shape["tile"]),
        mesh=mesh,
        in_specs=(
            P("half", None, "face", "tile"),
            P("half", None, "face", "tile"),
            P("half", "face", "tile", None, None),
            P("half", "face", "tile", None),
            P("half", "face", "tile", None, None),
            P("half", None, None),
            P("half", "face", "tile"),
            P("half", None, None),
            P("half", None, None),
            P("half", None, None),
            P("half", None),
        ),
        out_specs=(
            P("half", None, "face", "tile"),
            P("half", None, None),
            P("half", None, None),
            P("half", None, None),
            P("half", None),
        ),
        check_vma=False,
    )
```

```python
import functools
import math

import jax
import jax.numpy as jnp
import numpy as np
from jax import lax
from jax.experimental import pallas as pl
from jax.experimental.pallas import tpu as pltpu
from jax.sharding import PartitionSpec as P

CH = 64
CIN = 16
KC = 4
BS = 64
LANES = 128
GELU_C = math.sqrt(2.0 / math.pi)
BF = jnp.bfloat16
F32 = jnp.float32
MESH = pl.DeviceIdType.MESH
DIRS = [(-1, 0), (1, 0), (0, -1), (0, 1), (-1, -1), (-1, 1), (1, -1), (1, 1)]
OPP = [DIRS.index((-a, -b)) for a, b in DIRS]
N_EX = 5
EX_CH = (32, 128, 128, 64, 128)


def gelu_pair(pre):
    inner = jnp.tanh(GELU_C * (pre + 0.044715 * pre * pre * pre))
    value = 0.5 * pre * (1.0 + inner)
    slope = 0.5 * (1.0 + inner) + 0.5 * pre * (1.0 - inner * inner) * GELU_C * (
        1.0 + 3.0 * 0.044715 * pre * pre
    )
    return value, slope


def roll(x, shift):
    return pltpu.roll(x, shift % LANES, axis=1)


def lanes_of(rows):
    return lax.broadcasted_iota(jnp.int32, (rows, LANES), 1)


def barrel(x, amount, right):
    for bit in range(7):
        step = 1 << bit
        moved = roll(x, step if right else LANES - step)
        x = jnp.where((amount & step) != 0, moved, x)
    return x


def pair_sum(x):
    even = (lanes_of(x.shape[0]) & 1) == 0
    return x + jnp.where(even, roll(x, -1), roll(x, 1))


def edge_tables():
    place_fine = np.zeros((3, 16, LANES), np.float32)
    place_coarse = np.zeros((3, 16, LANES), np.float32)
    for a in range(3):
        for base, start in ((0, 0), (8, 64)):
            for r in range(4):
                place_fine[a, base + r + a, start + r] = 1
            for r in range(2):
                place_coarse[a, base + (0, 1, 3, 5)[r + a], start + r] = 1
    return place_fine, place_coarse


def first_tables():
    wide = CIN + KC
    tables = np.zeros((2, 9 * CH, LANES), np.float32)
    for k in range(9):
        for o in range(CH):
            for step in range(2):
                t = o * wide // LANES + step
                if t < CH * wide // LANES:
                    tables[step, k * CH + o, 8 * t + k if k < 8 else 80 + t] = 1
    return (tables,)


def conv_rows(weight, x_ref, outs, rows, step):
    z = jnp.dot(weight, x_ref[...], preferred_element_type=F32)
    lane = lanes_of(outs)
    halo_left = z[:outs, rows * LANES :]
    halo_right = z[2 * outs :, rows * LANES :]
    result = []
    for r in range(rows):
        at = slice(r * LANES, (r + 1) * LANES)
        left = jnp.where(lane < step, halo_left[:, r : r + 1], roll(z[:outs, at], step))
        right = jnp.where(
            lane >= LANES - step, halo_right[:, 64 + r : 65 + r], roll(z[2 * outs :, at], -step)
        )
        result.append(z[outs : 2 * outs, at] + left + right)
    return result


def weight_grad(delta_rows, x_ref, step):
    outs = delta_rows[0].shape[0]
    lane = lanes_of(outs)
    keep = (lane & (step - 1)) == 0
    zero = jnp.zeros((outs, LANES), F32)
    first, middle, last = [], [], []
    halo_left, halo_right = zero, zero
    for r, delta in enumerate(delta_rows):
        first.append(jnp.where(keep & (lane < LANES - step), roll(delta, -step), 0.0))
        middle.append(jnp.where(keep, delta, 0.0))
        last.append(jnp.where(keep & (lane >= step), roll(delta, step), 0.0))
        halo_left = jnp.where(lane == r, delta[:, 0:1], halo_left)
        halo_right = jnp.where(lane == 64 + r, delta[:, LANES - 1 : LANES], halo_right)
    parts = [first + [halo_left], middle + [zero], last + [halo_right]]
    stacked = jnp.concatenate(
        [jnp.concatenate(part, axis=1).astype(BF) for part in parts], axis=0
    )
    return lax.dot_general(
        stacked, x_ref[...], (((1,), (1,)), ((), ())), preferred_element_type=F32
    )


def kernel(
    nf,
    nt,
    na,
    nb,
    nc,
    state_hbm,
    cot_hbm,
    peer_hbm,
    src_hbm,
    tgt_hbm,
    interp_hbm,
    sea_hbm,
    w1_hbm,
    w2_hbm,
    w3_hbm,
    wo_hbm,
    find_hbm,
    placef_hbm,
    placec_hbm,
    pred_ref,
    gfirst_ref,
    gdown_ref,
    gup_ref,
    gout_ref,
    state_ref,
    cot_ref,
    peer_ref,
    src_ref,
    tgt_ref,
    interp_ref,
    sea_ref,
    w1_ref,
    w2_ref,
    w3_ref,
    wo_ref,
    find_ref,
    placef_ref,
    placec_ref,
    load_sem,
    s1,
    s2,
    s3,
    u2,
    u3,
    pred32,
    a1,
    a2,
    a3,
    b2,
    b3,
    outbox,
    inbox,
    row_send,
    row_recv,
    edge_send,
    edge_recv,
    x1,
    x2,
    x3,
    xd3,
    xd2,
    send_a,
    recv_a,
    part_a,
    zrecv_a,
    done_a,
    all_a,
    send_b,
    recv_b,
    part_b,
    zrecv_b,
    done_b,
    all_b,
    send_c,
    recv_c,
    part_c,
    zrecv_c,
    done_c,
    all_c,
    box_ssem,
    box_rsem,
    ex_ssem,
    ex_rsem,
    xy_ssem,
    xy_rsem,
    zs_ssem,
    zs_rsem,
    zg_ssem,
    zg_rsem,
    gx_ssem,
    gx_rsem,
    za_ssem,
    za_rsem,
):
    half = lax.axis_index("half")
    face = lax.axis_index("face")
    tile = lax.axis_index("tile")
    nz = nt // 2
    nxy = nf * 2
    y_hi = tile // nz
    z = tile % nz
    me_xy = face * 2 + y_hi

    def xy_peer(k):
        other = (me_xy + k) % nxy
        return other, {"face": other // 2, "tile": (other % 2) * nz + z}

    def z_peer(k):
        other = (z + k) % nz
        return other, {"tile": y_hi * nz + other}

    def box_peer(k):
        other = (tile + k) % nt
        return other, {"half": 1 - half, "tile": other}

    def neighbour(d):
        df, dt = DIRS[d]
        ok = (face + df >= 0) & (face + df < nf) & (tile + dt >= 0) & (tile + dt < nt)
        return ok, {"face": face + df, "tile": tile + dt}

    loads = [
        pltpu.make_async_copy(src, dst, load_sem.at[i])
        for i, (src, dst) in enumerate(
            (
                (state_hbm, state_ref),
                (peer_hbm, peer_ref),
                (src_hbm, src_ref),
                (w3_hbm, w3_ref),
                (w2_hbm, w2_ref),
                (w1_hbm, w1_ref),
                (find_hbm, find_ref),
                (wo_hbm, wo_ref),
                (tgt_hbm, tgt_ref),
                (interp_hbm, interp_ref),
                (sea_hbm, sea_ref),
                (cot_hbm, cot_ref),
                (placef_hbm, placef_ref),
                (placec_hbm, placec_ref),
            )
        )
    ]
    for load in loads:
        load.start()

    row_recv[...] = jnp.zeros_like(row_recv)
    edge_recv[...] = jnp.zeros_like(edge_recv)
    edge_send[...] = jnp.zeros_like(edge_send)

    barrier = pltpu.get_barrier_semaphore()

    def greet(peer, count):
        def body(k, carry):
            pl.semaphore_signal(barrier, inc=1, device_id=peer(k)[1], device_id_type=MESH)
            return carry

        lax.fori_loop(count[0], count[1], body, 0)

    greet(box_peer, (0, nt))
    greet(xy_peer, (1, nxy))
    greet(z_peer, (1, nz))
    expected = nt + nxy - 1 + nz - 1
    for d in range(8):
        ok, device = neighbour(d)
        expected = expected + ok.astype(jnp.int32)

        @pl.when(ok)
        def _(device=device):
            pl.semaphore_signal(barrier, inc=1, device_id=device, device_id_type=MESH)

    rows = 2 * nt * KC
    nblk = src_ref.shape[1]
    for load in loads[:3]:
        load.wait()
    state3 = state_ref[...].astype(F32)
    state_rows = [state3[:, q, :] for q in range(4)]
    peer_row = jnp.broadcast_to(peer_ref[...], (nblk, nblk))
    diagonal = lax.broadcasted_iota(jnp.int32, (nblk, nblk), 0) == lax.broadcasted_iota(
        jnp.int32, (nblk, nblk), 1
    )
    peer_col = jnp.sum(
        jnp.where(diagonal, peer_row, 0).astype(F32), axis=1, keepdims=True
    ).astype(jnp.int32)
    peer_row = peer_row[0:1]
    same = peer_col == peer_row
    earlier = lax.broadcasted_iota(jnp.int32, (nblk, nblk), 0) < lax.broadcasted_iota(
        jnp.int32, (nblk, nblk), 1
    )
    rank = jnp.sum(jnp.where(same & earlier, 1.0, 0.0), axis=0, keepdims=True)
    row_id = lax.broadcasted_iota(jnp.int32, (rows, nblk), 0)
    slot = (row_id // (nt * KC)).astype(F32)
    match = ((row_id // KC) % nt == peer_row) & (slot == rank)
    used = jnp.sum(jnp.where(match, 1.0, 0.0), axis=1, keepdims=True)
    start = jnp.sum(
        jnp.where(match, src_ref[...].astype(F32), 0.0), axis=1, keepdims=True
    ).astype(jnp.int32)
    start = jnp.broadcast_to(start, (rows, LANES))
    lane = lanes_of(rows)
    sub8 = lax.broadcasted_iota(jnp.int32, (8, LANES), 0)
    shift = start & (LANES - 1)
    from_tile = (start >> 7) + (lane < shift).astype(jnp.int32)
    window = jnp.zeros((rows, LANES), F32)
    for q in range(4):
        head = state_rows[q][0:8]
        head = jnp.where(sub8 < KC, head, pltpu.roll(head, 4, axis=0))
        window = jnp.where(
            from_tile == q, jnp.concatenate([head] * (rows // 8), axis=0), window
        )
    window = barrel(window, shift, False)
    window = jnp.where((lane < BS) & (used > 0.0), window, 0.0)
    packed = window[: rows // 2] + roll(window[rows // 2 :], BS)
    for p in range(nt):
        outbox[p] = packed[p * KC : (p + 1) * KC]

    loads[3].wait()
    for j in range(CH // 2):
        for t in range(3):
            at = 384 * j + 128 * t
            part = w3_ref[:, at : at + 128].astype(F32)
            s3[t, 8 * j : 8 * j + 8] = part[0:8]
            s3[t, 256 + j : 257 + j] = part[8:9]
    lane_j = lanes_of(CH // 2)
    for b in range(3):
        for a in range(3):
            k = 3 * a + b
            parts = [
                s3[t, pl.ds(k, CH // 2, stride=8), :] if k < 8 else s3[t, 256:288]
                for t in range(3)
            ]
            last = roll(parts[2], CH)
            u3[k, 0, pl.ds(0, CH // 2, stride=2), :] = parts[0]
            u3[k, 1, pl.ds(0, CH // 2, stride=2), :] = parts[1]
            u3[k, 0, pl.ds(1, CH // 2, stride=2), :] = jnp.where(
                lane_j < CH, roll(parts[1], CH), last
            )
            u3[k, 1, pl.ds(1, CH // 2, stride=2), :] = last
            tap = jnp.concatenate([u3[k, 0], u3[k, 1][:, 0:CH]], axis=1)
            a3[CH * b : CH * b + CH, 192 * a : 192 * a + 192] = tap.astype(BF)
            b3[192 * (2 - b) : 192 * (3 - b), CH * (2 - a) : CH * (3 - a)] = tap.T.astype(BF)

    pl.semaphore_wait(barrier, expected)

    def box_copy(k):
        other, device = box_peer(k)
        return pltpu.make_async_remote_copy(
            src_ref=outbox.at[other],
            dst_ref=inbox.at[tile],
            send_sem=box_ssem.at[k],
            recv_sem=box_rsem.at[tile],
            device_id=device,
            device_id_type=MESH,
        )

    def box_arrival(k):
        other, device = box_peer(k)
        return pltpu.make_async_remote_copy(
            src_ref=outbox.at[other],
            dst_ref=inbox.at[other],
            send_sem=box_ssem.at[k],
            recv_sem=box_rsem.at[other],
            device_id=device,
            device_id_type=MESH,
        )

    def each(low, high, act):
        def body(k, carry):
            act(k)
            return carry

        lax.fori_loop(low, high, body, 0)

    each(0, nt, lambda k: box_copy(k).start())

    for load in loads[4:]:
        load.wait()
    for j in range(CH):
        part = w2_ref[:, 128 * j : 128 * j + 128].astype(F32)
        s2[8 * j : 8 * j + 8] = part[0:8]
        s2[512 + j : 513 + j] = part[8:9]
    for b in range(3):
        for a in range(3):
            k = 3 * a + b
            part = s2[pl.ds(k, CH, stride=8), :] if k < 8 else s2[512:576]
            u2[k, pl.ds(0, CH, stride=2), :] = part
            u2[k, pl.ds(1, CH, stride=2), :] = roll(part, CH)
            tap = u2[k]
            a2[2 * CH * b : 2 * CH * b + 2 * CH, CH * a : CH * a + CH] = tap[
                :, 0:CH
            ].astype(BF)
            b2[CH * (2 - b) : CH * (3 - b), 2 * CH * (2 - a) : 2 * CH * (3 - a)] = tap.T[
                0:CH
            ].astype(BF)
    s1[...] = jnp.zeros_like(s1)
    for j in range(10):
        part = w1_ref[:, 128 * j : 128 * j + 128].astype(F32)
        s1[8 * j : 8 * j + 8] = part[0:8]
        s1[80 + j : 81 + j] = part[8:9]
    flat_first = s1[...].astype(BF)
    begins = jnp.dot(find_ref[0], flat_first, preferred_element_type=F32)
    follows = jnp.dot(find_ref[1], flat_first, preferred_element_type=F32)
    lane_first = lanes_of(9 * CH)
    offset = (
        (lax.broadcasted_iota(jnp.int32, (9 * CH, LANES), 0) % CH) * (CIN + KC)
    ) & (LANES - 1)
    taps = barrel(jnp.where(lane_first >= offset, begins, follows), offset, False)
    taps = jnp.where(lane_first < CIN + KC, taps, 0.0)
    for b in range(3):
        for a in range(3):
            k = 3 * a + b
            a1[CH * b : CH * b + CH, 32 * a : 32 * a + 32] = taps[
                CH * k : CH * k + CH, 0:32
            ].astype(BF)
    wo32 = jnp.zeros((16, LANES), F32)
    sub16 = lax.broadcasted_iota(jnp.int32, (16, LANES), 0)
    for j in range(CIN // 2):
        part = jnp.broadcast_to(
            wo_ref[0:1, LANES * j : LANES * j + LANES].astype(F32), (16, LANES)
        )
        wo32 = jnp.where(sub16 == 2 * j, part, wo32)
        wo32 = jnp.where(sub16 == 2 * j + 1, roll(part, CH), wo32)
    wo = wo32[:, 0:CH].astype(BF)
    wot = wo32.T[0:CH].astype(BF)
    zero64 = jnp.zeros((BS, BS), F32)
    one = interp_ref[...].astype(F32)
    matrix = jnp.concatenate(
        [jnp.concatenate([one, zero64], axis=1), jnp.concatenate([zero64, one], axis=1)], axis=0
    ).astype(BF)
    cot3 = cot_ref[...].astype(F32)
    cot = jnp.concatenate([cot3[:, q, :] for q in range(4)], axis=1).astype(BF)
    wanted = tgt_ref[...] & 511
    halves = jnp.concatenate([wanted >> 6, wanted & 63], axis=0).astype(F32).astype(BF)
    own_row = lax.broadcasted_iota(jnp.int32, (rows, nt), 0)
    own_peer = lax.broadcasted_iota(jnp.int32, (rows, nt), 1)
    copies = jnp.where((own_row // KC) % nt == own_peer, 1.0, 0.0).astype(BF)
    spots = lax.dot_general(
        copies, halves, (((1,), (1,)), ((), ())), preferred_element_type=F32
    )
    first_slot = lax.broadcasted_iota(jnp.int32, (rows, 1), 0) < nt * KC
    target = jnp.where(
        first_slot, spots[:, 0:1] * 64.0 + spots[:, 2:3], spots[:, 1:2] * 64.0 + spots[:, 3:4]
    ).astype(jnp.int32)

    def ex_copy(e, d, arrival):
        ok, device = neighbour(d)
        at = d if arrival else OPP[d]
        if d < 2:
            src = row_send.at[e, d, 0 : EX_CH[e]]
            dst = row_recv.at[e, at, 0 : EX_CH[e]]
        else:
            src = edge_send.at[e]
            dst = edge_recv.at[e, at - 2]
        return ok, pltpu.make_async_remote_copy(
            src_ref=src,
            dst_ref=dst,
            send_sem=ex_ssem.at[e, d],
            recv_sem=ex_rsem.at[e, at],
            device_id=device,
            device_id_type=MESH,
        )

    def ex_start(e):
        for d in range(8):
            ok, copy = ex_copy(e, d, False)
            pl.when(ok)(copy.start)

    def ex_wait(e):
        for d in range(8):
            ok, copy = ex_copy(e, d, True)

            @pl.when(ok)
            def _(copy=copy):
                copy.wait_recv()
                copy.wait_send()

    def edge_pick(rows_of):
        parts = []
        for targets in rows_of:
            right, left = sub16 < 0, sub16 < 0
            for j in targets:
                right, left = right | (sub16 == j), left | (sub16 == j + 8)
            hit = (right & (lane16 == LANES - 1)) | (left & (lane16 == 0))
            parts.append(jnp.where(hit, 1.0, 0.0))
        return jnp.concatenate(parts, axis=1).astype(BF)

    lane16 = lanes_of(16)
    pick_fine = edge_pick(((1, 5), (2,), (3,), (0, 4)))
    pick_coarse = edge_pick(((1, 2, 5), (0, 3, 4)))

    def pick(table, field):
        return lax.dot_general(
            table, field, (((1,), (1,)), ((), ())), preferred_element_type=F32
        ).astype(BF)

    takes = {
        2: (sub16 >= 1) & (sub16 <= 4),
        3: (sub16 >= 9) & (sub16 <= 12),
        4: sub16 == 0,
        5: sub16 == 8,
        6: sub16 == 5,
        7: sub16 == 13,
    }

    def halo_columns(e):
        held = jnp.zeros((16, LANES), F32)
        for d in range(2, 8):
            held = jnp.where(takes[d], edge_recv[e, d - 2].astype(F32), held)
        return held.T

    def place(columns, table_ref, a):
        return jnp.dot(
            columns.astype(BF), table_ref[a], preferred_element_type=F32
        ).astype(BF)

    def fill_centre(x_ref, chans, offset, total, field_rows):
        count = len(field_rows)
        for a in range(3):
            for r in range(count):
                if 1 <= r + a <= count:
                    x_ref[
                        a * total + offset : a * total + offset + chans,
                        r * LANES : (r + 1) * LANES,
                    ] = field_rows[r + a - 1]

    def fill_halo(x_ref, chans, offset, total, count, above, below, columns, table_ref):
        x_ref[offset : offset + chans, 0:LANES] = above
        x_ref[
            2 * total + offset : 2 * total + offset + chans, (count - 1) * LANES : count * LANES
        ] = below
        for a in range(3):
            x_ref[
                a * total + offset : a * total + offset + chans, count * LANES :
            ] = place(columns, table_ref, a)

    groups = (
        (na, send_a, recv_a, part_a, zrecv_a, done_a, all_a, 0),
        (nb, send_b, recv_b, part_b, zrecv_b, done_b, all_b, 2),
        (nc, send_c, recv_c, part_c, zrecv_c, done_c, all_c, 0),
    )

    def xy_copy(g, k, arrival):
        other, device = xy_peer(k)
        send, recv, m = groups[g][1], groups[g][2], 16 * groups[g][0]
        at = other if arrival else me_xy
        return pltpu.make_async_remote_copy(
            src_ref=send.at[pl.ds(pl.multiple_of(other * m, 16), m)],
            dst_ref=recv.at[at],
            send_sem=xy_ssem.at[g, k],
            recv_sem=xy_rsem.at[g, at],
            device_id=device,
            device_id_type=MESH,
        )

    def xy_start(g):
        each(1, nxy, lambda k: xy_copy(g, k, False).start())

    def z_owner(g, q):
        return (4 * q + groups[g][7]) % nz

    def zs_copy(g, q, source):
        n, send, recv, part, zrecv, done, full, first = groups[g]
        base = 0 if g == 0 else na
        return pltpu.make_async_remote_copy(
            src_ref=part.at[16 * q : 16 * q + 16],
            dst_ref=zrecv.at[q, source],
            send_sem=zs_ssem.at[base + q],
            recv_sem=zs_rsem.at[base + q, source],
            device_id={"tile": y_hi * nz + z_owner(g, q)},
            device_id_type=MESH,
        )

    def zg_copy(g, q, k):
        n, send, recv, part, zrecv, done, full, first = groups[g]
        base = 0 if g == 0 else na
        return pltpu.make_async_remote_copy(
            src_ref=done.at[16 * q : 16 * q + 16],
            dst_ref=done.at[16 * q : 16 * q + 16],
            send_sem=zg_ssem.at[base + q, k],
            recv_sem=zg_rsem.at[base + q],
            device_id=z_peer(k)[1],
            device_id_type=MESH,
        )

    def gx_copy(g, k, arrival):
        other, device = xy_peer(k)
        n, send, recv, part, zrecv, done, full, first = groups[g]
        m = 16 * n
        at = other if arrival else me_xy
        return pltpu.make_async_remote_copy(
            src_ref=done,
            dst_ref=full.at[pl.ds(pl.multiple_of(at * m, 16), m)],
            send_sem=gx_ssem.at[g, k],
            recv_sem=gx_rsem.at[g, at],
            device_id=device,
            device_id_type=MESH,
        )

    def zall_copy(k, arrival):
        other, device = z_peer(k)
        return pltpu.make_async_remote_copy(
            src_ref=part_c,
            dst_ref=zrecv_c.at[other if arrival else z],
            send_sem=za_ssem.at[k],
            recv_sem=za_rsem.at[other if arrival else z],
            device_id=device,
            device_id_type=MESH,
        )

    def stage_all_z():
        each(1, nz, lambda k: zall_copy(k, True).wait_recv())
        zrecv_c[z] = part_c[...]
        total = zrecv_c[0].astype(F32)
        for j in range(1, nz):
            total = total + zrecv_c[j].astype(F32)
        done_c[...] = total.astype(BF)
        each(1, nxy, lambda k: gx_copy(2, k, False).start())

    def stage_xy_to_z(g):
        n, send, recv, part, zrecv, done, full, first = groups[g]
        m = 16 * n
        total = send[pl.ds(pl.multiple_of(me_xy * m, 16), m), :].astype(F32)
        each(1, nxy, lambda k: xy_copy(g, k, True).wait_recv())
        recv[me_xy] = jnp.zeros((m, LANES), BF)
        for j in range(nxy):
            total = total + recv[j].astype(F32)
        part[...] = total.astype(BF)
        if g == 2:
            each(1, nz, lambda k: zall_copy(k, False).start())
            return
        for q in range(n):

            @pl.when(z != z_owner(g, q))
            def _(q=q):
                zs_copy(g, q, z).start()

    def stage_z_reduce(g):
        n, send, recv, part, zrecv, done, full, first = groups[g]
        for q in range(n):

            @pl.when(z == z_owner(g, q))
            def _(q=q):
                each(1, nz, lambda k: zs_copy(g, q, z_peer(k)[0]).wait_recv())
                zrecv[q, z] = part[16 * q : 16 * q + 16]
                total = jnp.zeros((16, LANES), F32)
                for j in range(nz):
                    total = total + zrecv[q, j].astype(F32)
                done[16 * q : 16 * q + 16] = total.astype(BF)
                each(1, nz, lambda k: zg_copy(g, q, k).start())

    def stage_z_to_xy(g):
        n, send, recv, part, zrecv, done, full, first = groups[g]
        for q in range(n):

            @pl.when(z != z_owner(g, q))
            def _(q=q):
                zg_copy(g, q, 1).wait_recv()

        each(1, nxy, lambda k: gx_copy(g, k, False).start())

    def stage_finish(g):
        n, send, recv, part, zrecv, done, full, first = groups[g]
        m = 16 * n
        each(1, nxy, lambda k: gx_copy(g, k, True).wait_recv())
        full[pl.ds(pl.multiple_of(me_xy * m, 16), m), :] = done[...]
        each(1, nxy, lambda k: xy_copy(g, k, False).wait_send())
        each(1, nxy, lambda k: gx_copy(g, k, False).wait_send())
        if g == 2:
            each(1, nz, lambda k: zall_copy(k, False).wait_send())
            return
        for q in range(n):

            @pl.when(z != z_owner(g, q))
            def _(q=q):
                zs_copy(g, q, z).wait_send()

            @pl.when(z == z_owner(g, q))
            def _(q=q):
                each(1, nz, lambda k: zg_copy(g, q, k).wait_send())

    target = jnp.broadcast_to(target, (rows, LANES))
    shift_in = target & (LANES - 1)
    to_tile = (target >> 7) + (lane < shift_in).astype(jnp.int32)
    each(0, nt, lambda k: box_arrival(k).wait_recv())
    arrived = jnp.concatenate([inbox[p] for p in range(nt)], axis=0)
    moved = jnp.dot(arrived.astype(BF), matrix, preferred_element_type=F32)
    lane_half = lanes_of(rows // 2)
    moved = jnp.concatenate(
        [
            jnp.where(lane_half < BS, moved, 0.0),
            roll(jnp.where(lane_half >= BS, moved, 0.0), BS),
        ],
        axis=0,
    )
    moved = barrel(moved, shift_in, True)
    lifted = []
    for q in range(4):
        chosen = jnp.where(to_tile == q, moved, 0.0)
        total = chosen[0:8]
        for i in range(1, rows // 8):
            total = total + chosen[8 * i : 8 * i + 8]
        total = total + pltpu.roll(total, 4, axis=0)
        total = total * sea_ref[q : q + 1, :].astype(F32)
        forcing = jnp.concatenate(
            [jnp.where(sub8 < KC, total, 0.0), jnp.zeros((8, LANES), F32)], axis=0
        ).astype(BF)
        lifted.append(
            jnp.concatenate([state_rows[q].astype(BF), forcing], axis=0)
        )

    row_send[0, 0, 0:32] = lifted[0]
    row_send[0, 1, 0:32] = lifted[3]
    edge_send[0, :, 0:32] = pick(pick_fine, jnp.concatenate(lifted, axis=1))
    ex_start(0)
    fill_centre(x1, 32, 0, 32, lifted)
    ex_wait(0)
    columns = halo_columns(0)[0:32]
    fill_halo(
        x1, 32, 0, 32, 4, row_recv[0, 0, 0:32], row_recv[0, 1, 0:32], columns, placef_ref
    )
    pre = conv_rows(a1[...], x1, CH, 4, 1)
    hidden_one, slope_one = [], []
    for r in range(4):
        value, slope = gelu_pair(pre[r])
        hidden_one.append(value.astype(BF))
        slope_one.append(slope)
    pooled = [
        (
            pair_sum(hidden_one[2 * r].astype(F32) + hidden_one[2 * r + 1].astype(F32)) * 0.25
        ).astype(BF)
        for r in range(2)
    ]

    for at, fine, coarse in ((0, 0, 0), (1, 3, 1)):
        row_send[1, at, 0:CH] = hidden_one[fine]
        row_send[1, at, CH : 2 * CH] = pooled[coarse]
    edge_send[1] = jnp.concatenate(
        [
            pick(pick_fine, jnp.concatenate(hidden_one, axis=1)),
            pick(pick_coarse, jnp.concatenate(pooled, axis=1)),
        ],
        axis=1,
    )
    ex_start(1)
    fill_centre(x3, CH, 0, 3 * CH, hidden_one)
    fill_centre(x2, CH, 0, CH, pooled)
    ex_wait(1)
    columns = halo_columns(1)
    fill_halo(
        x2,
        CH,
        0,
        CH,
        2,
        row_recv[1, 0, CH : 2 * CH],
        row_recv[1, 1, CH : 2 * CH],
        columns[CH : 2 * CH],
        placec_ref,
    )
    pre = conv_rows(a2[...], x2, 2 * CH, 2, 2)
    hidden_two, slope_two = [], []
    for r in range(2):
        value, slope = gelu_pair(pre[r])
        hidden_two.append(value.astype(BF))
        slope_two.append(slope)

    row_send[2, 0] = hidden_two[0]
    row_send[2, 1] = hidden_two[1]
    edge_send[2] = pick(pick_coarse, jnp.concatenate(hidden_two, axis=1))
    ex_start(2)
    fill_halo(
        x3, CH, 0, 3 * CH, 4, row_recv[1, 0, 0:CH], row_recv[1, 1, 0:CH], columns[0:CH], placef_ref
    )
    fill_centre(x3, 2 * CH, CH, 3 * CH, [hidden_two[r // 2] for r in range(4)])
    back_three = jnp.dot(wot, cot, preferred_element_type=F32)
    ex_wait(2)
    columns = halo_columns(2)
    fill_halo(
        x3, 2 * CH, CH, 3 * CH, 4, row_recv[2, 0], row_recv[2, 1], columns, placef_ref
    )
    pre = conv_rows(a3[...], x3, CH, 4, 1)
    hidden_three, delta_three = [], []
    for r in range(4):
        value, slope = gelu_pair(pre[r])
        hidden_three.append(value.astype(BF))
        delta_three.append(
            (back_three[:, r * LANES : (r + 1) * LANES] * slope).astype(BF)
        )

    row_send[3, 0, 0:CH] = delta_three[0]
    row_send[3, 1, 0:CH] = delta_three[3]
    edge_send[3, :, 0:CH] = pick(pick_fine, jnp.concatenate(delta_three, axis=1))
    ex_start(3)
    fill_centre(xd3, CH, 0, CH, delta_three)
    flat_three = jnp.concatenate(hidden_three, axis=1)
    change = jnp.dot(wo, flat_three, preferred_element_type=F32)
    for r in range(4):
        pred32[:, r, :] = state_rows[r] + change[:, r * LANES : (r + 1) * LANES]
    pred_ref[...] = pred32[...].astype(BF)
    grad_out = lax.dot_general(
        cot, flat_three, (((1,), (1,)), ((), ())), preferred_element_type=F32
    )
    grad_up = weight_grad([d.astype(F32) for d in delta_three], x3, 1)
    tiles = [grad_up[:, LANES * t : LANES * t + LANES] for t in range(4)]
    tiles.append(jnp.concatenate([grad_up[:, 512:576], jnp.zeros((192, CH), F32)], axis=1))
    lane_up = lanes_of(192)
    second = roll(tiles[2], CH)
    starts = (
        (tiles[0], tiles[1]),
        (jnp.where(lane_up < CH, roll(tiles[1], CH), second), second),
        (tiles[3], tiles[4]),
    )
    for a in range(3):
        for t in range(2):
            u3[3 * a, t] = starts[a][t][0:CH]
            u3[3 * a + 1, t] = starts[a][t][CH : 2 * CH]
            u3[3 * a + 2, t] = starts[a][t][2 * CH : 3 * CH]
    for k in range(9):
        even = [u3[k, t, pl.ds(0, CH // 2, stride=2), :] for t in range(2)]
        uneven = [roll(u3[k, t, pl.ds(1, CH // 2, stride=2), :], CH) for t in range(2)]
        pairs = (
            even[0],
            jnp.where(lane_j < CH, even[1], uneven[0]),
            jnp.where(lane_j < CH, uneven[0], uneven[1]),
        )
        for t in range(3):
            at = 32 * (9 * t + k)
            send_a[at : at + 32] = pairs[t].astype(BF)
    send_a[864:880] = jnp.concatenate([grad_out, jnp.zeros((16, 64), F32)], axis=1).astype(BF)
    if 16 * na * nxy > 880:
        send_a[880:] = jnp.zeros((16 * na * nxy - 880, LANES), BF)
    xy_start(0)
    ex_wait(3)
    columns = halo_columns(3)[0:CH]
    fill_halo(
        xd3, CH, 0, CH, 4, row_recv[3, 0, 0:CH], row_recv[3, 1, 0:CH], columns, placef_ref
    )
    join = conv_rows(b3[...], xd3, 3 * CH, 4, 1)
    delta_two = [
        (pair_sum(join[2 * r][CH:] + join[2 * r + 1][CH:]) * slope_two[r]).astype(BF)
        for r in range(2)
    ]

    row_send[4, 0] = delta_two[0]
    row_send[4, 1] = delta_two[1]
    edge_send[4] = pick(pick_coarse, jnp.concatenate(delta_two, axis=1))
    ex_start(4)
    fill_centre(xd2, 2 * CH, 0, 2 * CH, delta_two)
    grad_down = weight_grad([d.astype(F32) for d in delta_two], x2, 2)
    lane_down = lanes_of(CH)
    right = jnp.concatenate([grad_down[:, 128:192], jnp.zeros((384, CH), F32)], axis=1)
    for b in range(3):
        u2[b] = grad_down[2 * CH * b : 2 * CH * b + 2 * CH, 0:LANES]
        u2[3 + b] = right[2 * CH * b : 2 * CH * b + 2 * CH]
    for b in range(3):
        for a in range(3):
            even = u2[3 * (a // 2) + b, pl.ds(0, CH, stride=2), :]
            uneven = u2[3 * (a // 2) + b, pl.ds(1, CH, stride=2), :]
            if a == 1:
                pair = jnp.where(lane_down < CH, roll(even, CH), uneven)
            else:
                pair = jnp.where(lane_down < CH, even, roll(uneven, CH))
            at = CH * (3 * a + b)
            send_b[at : at + CH] = pair.astype(BF)
    if 16 * nb * nxy > 576:
        send_b[576:] = jnp.zeros((16 * nb * nxy - 576, LANES), BF)
    xy_start(1)
    stage_xy_to_z(0)
    ex_wait(4)
    columns = halo_columns(4)
    fill_halo(
        xd2, 2 * CH, 0, 2 * CH, 2, row_recv[4, 0], row_recv[4, 1], columns, placec_ref
    )
    d_pool = conv_rows(b2[...], xd2, CH, 2, 2)
    delta_one = [
        ((join[r][0:CH] + 0.25 * d_pool[r // 2]) * slope_one[r]).astype(BF).astype(F32)
        for r in range(4)
    ]
    grad_first = weight_grad(delta_one, x1, 1)
    send_c[0:192] = jnp.concatenate([grad_first, jnp.zeros((192, 32), F32)], axis=1).astype(BF)
    if 16 * nc * nxy > 192:
        send_c[192:] = jnp.zeros((16 * nc * nxy - 192, LANES), BF)
    xy_start(2)
    stage_xy_to_z(1)
    stage_z_reduce(0)
    stage_xy_to_z(2)
    stage_z_reduce(1)
    stage_z_to_xy(0)
    stage_all_z()
    stage_z_to_xy(1)
    scale = 1.0 / math.sqrt(nf * 4 * nt * LANES)
    stage_finish(0)
    for t in range(3):
        for k in range(9):
            at = 32 * (9 * t + k)
            part = all_a[at : at + 32].astype(F32) * scale
            if k < 8:
                s3[t, pl.ds(k, CH // 2, stride=8), :] = part
            else:
                s3[t, 256:288] = part
    for j in range(CH // 2):
        for t in range(3):
            at = 384 * j + 128 * t
            gup_ref[0:8, at : at + 128] = s3[t, 8 * j : 8 * j + 8]
            gup_ref[8:9, at : at + 128] = s3[t, 256 + j : 257 + j]
    part = all_a[864:880].astype(F32) * scale
    turned = roll(part, CH)
    lane1 = lanes_of(1)
    for j in range(CIN // 2):
        gout_ref[0:1, LANES * j : LANES * j + LANES] = jnp.where(
            lane1 < CH, part[2 * j : 2 * j + 1], turned[2 * j + 1 : 2 * j + 2]
        )
    stage_finish(2)
    sums = all_c[0:192].astype(F32)
    taps = jnp.concatenate(
        [
            roll(sums[CH * b : CH * b + CH], -32 * a) if a else sums[CH * b : CH * b + CH]
            for a in range(3)
            for b in range(3)
        ],
        axis=0,
    )
    taps = barrel(jnp.where(lane_first < CIN + KC, taps, 0.0), offset, True)
    flat_first = sum(
        lax.dot_general(
            find_ref[step],
            jnp.where((lane_first >= offset) == (step == 0), taps, 0.0).astype(BF),
            (((0,), (0,)), ((), ())),
            preferred_element_type=F32,
        )
        for step in range(2)
    )
    for j in range(10):
        gfirst_ref[0:8, 128 * j : 128 * j + 128] = flat_first[8 * j : 8 * j + 8] * scale
        gfirst_ref[8:9, 128 * j : 128 * j + 128] = flat_first[80 + j : 81 + j] * scale
    stage_finish(1)
    for k in range(9):
        part = all_b[CH * k : CH * k + CH].astype(F32) * scale
        if k < 8:
            s2[pl.ds(k, CH, stride=8), :] = part
        else:
            s2[512:576] = part
    for j in range(CH):
        gdown_ref[0:8, 128 * j : 128 * j + 128] = s2[8 * j : 8 * j + 8]
        gdown_ref[8:9, 128 * j : 128 * j + 128] = s2[512 + j : 513 + j]
    each(0, nt, lambda k: box_copy(k).wait_send())


def local(
    nf,
    nt,
    state,
    cotangent,
    block_peer,
    source_start,
    target_start,
    interp,
    sea_mask,
    w_first,
    w_down,
    w_up,
    w_out,
):
    nxy, nz = nf * 2, nt // 2
    na, nb, nc = -(-55 // nxy), -(-36 // nxy), -(-12 // nxy)
    nblk = source_start.shape[-1]
    tables = [jnp.asarray(table, BF) for table in first_tables() + edge_tables()]
    operands = (
        state[0],
        cotangent[0],
        block_peer.reshape(1, nblk),
        source_start.reshape(1, nblk),
        target_start.reshape(nt, 2).T,
        interp[0],
        sea_mask[0],
        w_first[0],
        w_down[0],
        w_up[0],
        w_out,
        *tables,
    )
    dma = pltpu.SemaphoreType.DMA
    scratch = [pltpu.VMEM(op.shape, op.dtype) for op in operands]
    scratch += [
        dma((len(operands),)),
        pltpu.VMEM((LANES, LANES), F32),
        pltpu.VMEM((576, LANES), F32),
        pltpu.VMEM((3, 288, LANES), F32),
        pltpu.VMEM((9, 2 * CH, LANES), F32),
        pltpu.VMEM((9, 2, CH, LANES), F32),
        pltpu.VMEM((CIN, 4, LANES), F32),
        pltpu.VMEM((3 * CH, 96), BF),
        pltpu.VMEM((6 * CH, 3 * CH), BF),
        pltpu.VMEM((3 * CH, 9 * CH), BF),
        pltpu.VMEM((3 * CH, 6 * CH), BF),
        pltpu.VMEM((9 * CH, 3 * CH), BF),
        pltpu.VMEM((nt, KC, LANES), F32),
        pltpu.VMEM((nt, KC, LANES), F32),
        pltpu.VMEM((N_EX, 2, LANES, LANES), BF),
        pltpu.VMEM((N_EX, 2, LANES, LANES), BF),
        pltpu.VMEM((N_EX, 16, LANES), BF),
        pltpu.VMEM((N_EX, 6, 16, LANES), BF),
        pltpu.VMEM((96, 5 * LANES), BF),
        pltpu.VMEM((3 * CH, 3 * LANES), BF),
        pltpu.VMEM((9 * CH, 5 * LANES), BF),
        pltpu.VMEM((3 * CH, 5 * LANES), BF),
        pltpu.VMEM((6 * CH, 3 * LANES), BF),
    ]
    for n in (na, nb, nc):
        scratch += [
            pltpu.VMEM((nxy * n * 16, LANES), BF),
            pltpu.VMEM((nxy, n * 16, LANES), BF),
            pltpu.VMEM((n * 16, LANES), BF),
            pltpu.VMEM((nz, n * 16, LANES) if n == nc else (n, nz, 16, LANES), BF),
            pltpu.VMEM((n * 16, LANES), BF),
            pltpu.VMEM((nxy * n * 16, LANES), BF),
        ]
    scratch += [
        dma((nt,)),
        dma((nt,)),
        dma((N_EX, 8)),
        dma((N_EX, 8)),
        dma((3, nxy)),
        dma((3, nxy)),
        dma((na + nb,)),
        dma((na + nb, nz)),
        dma((na + nb, nz)),
        dma((na + nb,)),
        dma((3, nxy)),
        dma((3, nxy)),
        dma((nz,)),
        dma((nz,)),
    ]
    vmem = pl.BlockSpec(memory_space=pltpu.VMEM)
    predicted, grad_first, grad_down, grad_up, grad_out = pl.pallas_call(
        functools.partial(kernel, nf, nt, na, nb, nc),
        out_shape=(
            jax.ShapeDtypeStruct((CIN, 4, LANES), BF),
            jax.ShapeDtypeStruct(w_first.shape[1:], F32),
            jax.ShapeDtypeStruct(w_down.shape[1:], F32),
            jax.ShapeDtypeStruct(w_up.shape[1:], F32),
            jax.ShapeDtypeStruct(w_out.shape, F32),
        ),
        in_specs=[pl.BlockSpec(memory_space=pltpu.HBM)] * len(operands),
        out_specs=(vmem,) * 5,
        scratch_shapes=scratch,
        compiler_params=pltpu.CompilerParams(
            collective_id=0, has_side_effects=True, vmem_limit_bytes=64 * 2**20
        ),
    )(*operands)

    return predicted[None], grad_first[None], grad_down[None], grad_up[None], grad_out


def solution(mesh):
    return jax.shard_map(
        functools.partial(local, mesh.shape["face"], mesh.shape["tile"]),
        mesh=mesh,
        in_specs=(
            P("half", None, "face", "tile"),
            P("half", None, "face", "tile"),
            P("half", "face", "tile", None, None),
            P("half", "face", "tile", None),
            P("half", "face", "tile", None, None),
            P("half", None, None),
            P("half", "face", "tile"),
            P("half", None, None),
            P("half", None, None),
            P("half", None, None),
            P("half", None),
        ),
        out_specs=(
            P("half", None, "face", "tile"),
            P("half", None, None),
            P("half", None, None),
            P("half", None, None),
            P("half", None),
        ),
        check_vma=False,
    )
```

```python
import functools
import math

import jax
import jax.numpy as jnp
import numpy as np
from jax import lax
from jax.experimental import pallas as pl
from jax.experimental.pallas import tpu as pltpu
from jax.sharding import PartitionSpec as P

CH = 64
CIN = 16
KC = 4
BS = 64
LANES = 128
GELU_C = math.sqrt(2.0 / math.pi)
BF = jnp.bfloat16
F32 = jnp.float32
MESH = pl.DeviceIdType.MESH
DIRS = [(-1, 0), (1, 0), (0, -1), (0, 1), (-1, -1), (-1, 1), (1, -1), (1, 1)]
OPP = [DIRS.index((-a, -b)) for a, b in DIRS]
WIDE_CH = (32, CH)
PITCH = 6


def fine_lanes(r):
    return PITCH * (r + 3) + 2, 64 + PITCH * (r + 3) + 3


def coarse_lanes(r):
    return PITCH * (2 * r + 3) + 1, 64 + PITCH * (2 * r + 3) + 3


def gelu_pair(pre):
    inner = jnp.tanh(GELU_C * (pre + 0.044715 * pre * pre * pre))
    value = 0.5 * pre * (1.0 + inner)
    slope = 0.5 * (1.0 + inner) + 0.5 * pre * (1.0 - inner * inner) * GELU_C * (
        1.0 + 3.0 * 0.044715 * pre * pre
    )
    return value, slope


def roll(x, shift):
    return pltpu.roll(x, shift % LANES, axis=1)


def lanes_of(rows):
    return lax.broadcasted_iota(jnp.int32, (rows, LANES), 1)


def barrel(x, amount, right):
    for bit in range(7):
        step = 1 << bit
        moved = roll(x, step if right else LANES - step)
        x = jnp.where((amount & step) != 0, moved, x)
    return x


def pair_sum(x):
    even = (lanes_of(x.shape[0]) & 1) == 0
    return x + jnp.where(even, roll(x, -1), roll(x, 1))


def edge_tables():
    place = np.zeros((4, 16, LANES), np.float32)
    for r in range(4):
        for side in range(2):
            for a in range(3):
                place[a, 8 * side + r + a, fine_lanes(r)[side]] = 1
            place[3, 8 * side + (0, 1, 3, 5)[r], coarse_lanes(r - 1)[side]] = 1
    panel = np.zeros((9, 32, LANES), np.float32)
    for side in range(2):
        for row in range(-3, 7):
            for c in range(6):
                df = -1 if row < 0 else int(row > 3)
                dt = (-1 if c < 3 else 0) if side == 0 else int(c >= 3)
                source = 8 if (df, dt) == (0, 0) else DIRS.index((df, dt))
                panel[source, 8 * (row - 4 * df) + (c + 3) % 6, 64 * side + PITCH * (row + 3) + c] = 1
    return place, panel.reshape(288, LANES)


def first_tables():
    wide = CIN + KC
    tables = np.zeros((2, 9 * CH, LANES), np.float32)
    for k in range(9):
        for o in range(CH):
            for step in range(2):
                t = o * wide // LANES + step
                if t < CH * wide // LANES:
                    tables[step, k * CH + o, 8 * t + k if k < 8 else 80 + t] = 1
    return (tables,)


def conv_rows(weight, x_ref, outs, rows, step, halo_lanes):
    z = jnp.dot(weight, x_ref[...], preferred_element_type=F32)
    lane = lanes_of(outs)
    halo_left = z[:outs, rows * LANES :]
    halo_right = z[2 * outs :, rows * LANES :]
    result = []
    for r in range(rows):
        at = slice(r * LANES, (r + 1) * LANES)
        on_left, on_right = halo_lanes(r)
        left = jnp.where(
            lane < step, halo_left[:, on_left : on_left + 1], roll(z[:outs, at], step)
        )
        right = jnp.where(
            lane >= LANES - step,
            halo_right[:, on_right : on_right + 1],
            roll(z[2 * outs :, at], -step),
        )
        result.append(z[outs : 2 * outs, at] + left + right)
    panel = z[outs : 2 * outs, rows * LANES :] + roll(halo_left, 1) + roll(halo_right, -1)
    return result, panel


def weight_grad(delta_rows, field, step, halo_lanes):
    outs = delta_rows[0].shape[0]
    lane = lanes_of(outs)
    keep = (lane & (step - 1)) == 0
    zero = jnp.zeros((outs, LANES), F32)
    first, middle, last = [], [], []
    halo_left, halo_right = zero, zero
    for r, delta in enumerate(delta_rows):
        first.append(jnp.where(keep & (lane < LANES - step), roll(delta, -step), 0.0))
        middle.append(jnp.where(keep, delta, 0.0))
        last.append(jnp.where(keep & (lane >= step), roll(delta, step), 0.0))
        on_left, on_right = halo_lanes(r)
        halo_left = jnp.where(lane == on_left, delta[:, 0:1], halo_left)
        halo_right = jnp.where(lane == on_right, delta[:, LANES - 1 : LANES], halo_right)
    parts = [first + [halo_left], middle + [zero], last + [halo_right]]
    stacked = jnp.concatenate(
        [jnp.concatenate(part, axis=1).astype(BF) for part in parts], axis=0
    )
    return lax.dot_general(
        stacked, field, (((1,), (1,)), ((), ())), preferred_element_type=F32
    )


def kernel(
    nf,
    nt,
    na,
    nb,
    nc,
    state_hbm,
    cot_hbm,
    peer_hbm,
    src_hbm,
    tgt_hbm,
    interp_hbm,
    sea_hbm,
    w1_hbm,
    w2_hbm,
    w3_hbm,
    wo_hbm,
    find_hbm,
    place_hbm,
    panel_hbm,
    pred_ref,
    gfirst_ref,
    gdown_ref,
    gup_ref,
    gout_ref,
    state_ref,
    cot_ref,
    peer_ref,
    src_ref,
    tgt_ref,
    interp_ref,
    sea_ref,
    w1_ref,
    w2_ref,
    w3_ref,
    wo_ref,
    find_ref,
    place_ref,
    panel_ref,
    load_sem,
    s1,
    s2,
    s3,
    u2,
    u3,
    pred32,
    a1,
    a2,
    a3,
    b2,
    b3,
    outbox,
    inbox,
    row_send,
    row_recv,
    edge_send,
    edge_recv,
    wide_own,
    wide_recv,
    rim_send,
    rim_recv,
    x1,
    x2,
    x3,
    xd3,
    xd2,
    send_a,
    recv_a,
    part_a,
    zrecv_a,
    done_a,
    all_a,
    send_b,
    recv_b,
    part_b,
    zrecv_b,
    done_b,
    all_b,
    send_c,
    recv_c,
    part_c,
    zrecv_c,
    done_c,
    all_c,
    box_ssem,
    box_rsem,
    ex_ssem,
    ex_rsem,
    wide_ssem,
    wide_rsem,
    xy_ssem,
    xy_rsem,
    zs_ssem,
    zs_rsem,
    zg_ssem,
    zg_rsem,
    gx_ssem,
    gx_rsem,
    za_ssem,
    za_rsem,
):
    half = lax.axis_index("half")
    face = lax.axis_index("face")
    tile = lax.axis_index("tile")
    nz = nt // 2
    nxy = nf * 2
    y_hi = tile // nz
    z = tile % nz
    me_xy = face * 2 + y_hi

    def xy_peer(k):
        other = (me_xy + k) % nxy
        return other, {"face": other // 2, "tile": (other % 2) * nz + z}

    def z_peer(k):
        other = (z + k) % nz
        return other, {"tile": y_hi * nz + other}

    def box_peer(k):
        other = (tile + k) % nt
        return other, {"half": 1 - half, "tile": other}

    def neighbour(d):
        df, dt = DIRS[d]
        ok = (face + df >= 0) & (face + df < nf) & (tile + dt >= 0) & (tile + dt < nt)
        return ok, {"face": face + df, "tile": tile + dt}

    loads = [
        pltpu.make_async_copy(src, dst, load_sem.at[i])
        for i, (src, dst) in enumerate(
            (
                (state_hbm, state_ref),
                (peer_hbm, peer_ref),
                (src_hbm, src_ref),
                (w3_hbm, w3_ref),
                (w2_hbm, w2_ref),
                (w1_hbm, w1_ref),
                (find_hbm, find_ref),
                (wo_hbm, wo_ref),
                (tgt_hbm, tgt_ref),
                (interp_hbm, interp_ref),
                (sea_hbm, sea_ref),
                (cot_hbm, cot_ref),
                (place_hbm, place_ref),
                (panel_hbm, panel_ref),
            )
        )
    ]
    barrier = pltpu.get_barrier_semaphore()

    def greet(peer, count):
        def body(k, carry):
            pl.semaphore_signal(barrier, inc=1, device_id=peer(k)[1], device_id_type=MESH)
            return carry

        lax.fori_loop(count[0], count[1], body, 0)

    far_first = sorted(range(nt), key=lambda k: -min(k % nz, nz - k % nz))
    for k in far_first:
        pl.semaphore_signal(barrier, inc=1, device_id=box_peer(k)[1], device_id_type=MESH)
    row_recv[...] = jnp.zeros_like(row_recv)
    edge_recv[...] = jnp.zeros_like(edge_recv)
    wide_recv[...] = jnp.zeros_like(wide_recv)
    rim_recv[...] = jnp.zeros_like(rim_recv)
    rim_send[...] = jnp.zeros_like(rim_send)
    greet(xy_peer, (1, nxy))
    greet(z_peer, (1, nz))
    expected = nt + nxy - 1 + nz - 1
    for d in range(8):
        ok, device = neighbour(d)
        expected = expected + ok.astype(jnp.int32)

        @pl.when(ok)
        def _(device=device):
            pl.semaphore_signal(barrier, inc=1, device_id=device, device_id_type=MESH)

    for load in loads:
        load.start()

    rows = 2 * nt * KC
    nblk = src_ref.shape[1]
    for load in loads[:3]:
        load.wait()
    state3 = state_ref[...].astype(F32)
    state_rows = [state3[:, q, :] for q in range(4)]
    peer_row = jnp.broadcast_to(peer_ref[...], (nblk, nblk))
    diagonal = lax.broadcasted_iota(jnp.int32, (nblk, nblk), 0) == lax.broadcasted_iota(
        jnp.int32, (nblk, nblk), 1
    )
    peer_col = jnp.sum(
        jnp.where(diagonal, peer_row, 0).astype(F32), axis=1, keepdims=True
    ).astype(jnp.int32)
    peer_row = peer_row[0:1]
    same = peer_col == peer_row
    earlier = lax.broadcasted_iota(jnp.int32, (nblk, nblk), 0) < lax.broadcasted_iota(
        jnp.int32, (nblk, nblk), 1
    )
    rank = jnp.sum(jnp.where(same & earlier, 1.0, 0.0), axis=0, keepdims=True)
    row_id = lax.broadcasted_iota(jnp.int32, (rows, nblk), 0)
    slot = (row_id // (nt * KC)).astype(F32)
    match = ((row_id // KC) % nt == peer_row) & (slot == rank)
    used = jnp.sum(jnp.where(match, 1.0, 0.0), axis=1, keepdims=True)
    start = jnp.sum(
        jnp.where(match, src_ref[...].astype(F32), 0.0), axis=1, keepdims=True
    ).astype(jnp.int32)
    start = jnp.broadcast_to(start, (rows, LANES))
    lane = lanes_of(rows)
    sub8 = lax.broadcasted_iota(jnp.int32, (8, LANES), 0)
    shift = start & (LANES - 1)
    from_tile = (start >> 7) + (lane < shift).astype(jnp.int32)
    window = jnp.zeros((rows, LANES), F32)
    for q in range(4):
        head = state_rows[q][0:8]
        head = jnp.where(sub8 < KC, head, pltpu.roll(head, 4, axis=0))
        window = jnp.where(
            from_tile == q, jnp.concatenate([head] * (rows // 8), axis=0), window
        )
    window = barrel(window, shift, False)
    window = jnp.where((lane < BS) & (used > 0.0), window, 0.0)
    packed = window[: rows // 2] + roll(window[rows // 2 :], BS)
    for p in range(nt):
        outbox[p] = packed[p * KC : (p + 1) * KC]

    loads[3].wait()
    for j in range(CH // 2):
        for t in range(3):
            at = 384 * j + 128 * t
            part = w3_ref[:, at : at + 128].astype(F32)
            s3[t, 8 * j : 8 * j + 8] = part[0:8]
            s3[t, 256 + j : 257 + j] = part[8:9]
    lane_j = lanes_of(CH // 2)
    for b in range(3):
        for a in range(3):
            k = 3 * a + b
            parts = [
                s3[t, pl.ds(k, CH // 2, stride=8), :] if k < 8 else s3[t, 256:288]
                for t in range(3)
            ]
            last = roll(parts[2], CH)
            u3[k, 0, pl.ds(0, CH // 2, stride=2), :] = parts[0]
            u3[k, 1, pl.ds(0, CH // 2, stride=2), :] = parts[1]
            u3[k, 0, pl.ds(1, CH // 2, stride=2), :] = jnp.where(
                lane_j < CH, roll(parts[1], CH), last
            )
            u3[k, 1, pl.ds(1, CH // 2, stride=2), :] = last
            tap = jnp.concatenate([u3[k, 0], u3[k, 1][:, 0:CH]], axis=1)
            a3[CH * b : CH * b + CH, 192 * a : 192 * a + 192] = tap.astype(BF)
            b3[192 * (2 - b) : 192 * (3 - b), CH * (2 - a) : CH * (3 - a)] = tap.T.astype(BF)

    pl.semaphore_wait(barrier, expected)

    def box_copy(k):
        other, device = box_peer(k)
        return pltpu.make_async_remote_copy(
            src_ref=outbox.at[other],
            dst_ref=inbox.at[tile],
            send_sem=box_ssem.at[k],
            recv_sem=box_rsem.at[tile],
            device_id=device,
            device_id_type=MESH,
        )

    def box_arrival(k):
        other, device = box_peer(k)
        return pltpu.make_async_remote_copy(
            src_ref=outbox.at[other],
            dst_ref=inbox.at[other],
            send_sem=box_ssem.at[k],
            recv_sem=box_rsem.at[other],
            device_id=device,
            device_id_type=MESH,
        )

    def each(low, high, act):
        def body(k, carry):
            act(k)
            return carry

        lax.fori_loop(low, high, body, 0)

    for k in far_first:
        box_copy(k).start()

    for load in loads[4:]:
        load.wait()
    for j in range(CH):
        part = w2_ref[:, 128 * j : 128 * j + 128].astype(F32)
        s2[8 * j : 8 * j + 8] = part[0:8]
        s2[512 + j : 513 + j] = part[8:9]
    for b in range(3):
        for a in range(3):
            k = 3 * a + b
            part = s2[pl.ds(k, CH, stride=8), :] if k < 8 else s2[512:576]
            u2[k, pl.ds(0, CH, stride=2), :] = part
            u2[k, pl.ds(1, CH, stride=2), :] = roll(part, CH)
            tap = u2[k]
            a2[2 * CH * b : 2 * CH * b + 2 * CH, CH * a : CH * a + CH] = tap[
                :, 0:CH
            ].astype(BF)
            b2[CH * (2 - b) : CH * (3 - b), 2 * CH * (2 - a) : 2 * CH * (3 - a)] = tap.T[
                0:CH
            ].astype(BF)
    s1[...] = jnp.zeros_like(s1)
    for j in range(10):
        part = w1_ref[:, 128 * j : 128 * j + 128].astype(F32)
        s1[8 * j : 8 * j + 8] = part[0:8]
        s1[80 + j : 81 + j] = part[8:9]
    flat_first = s1[...].astype(BF)
    begins = jnp.dot(find_ref[0], flat_first, preferred_element_type=F32)
    follows = jnp.dot(find_ref[1], flat_first, preferred_element_type=F32)
    lane_first = lanes_of(9 * CH)
    offset = (
        (lax.broadcasted_iota(jnp.int32, (9 * CH, LANES), 0) % CH) * (CIN + KC)
    ) & (LANES - 1)
    taps = barrel(jnp.where(lane_first >= offset, begins, follows), offset, False)
    taps = jnp.where(lane_first < CIN + KC, taps, 0.0)
    for b in range(3):
        for a in range(3):
            k = 3 * a + b
            a1[CH * b : CH * b + CH, 32 * a : 32 * a + 32] = taps[
                CH * k : CH * k + CH, 0:32
            ].astype(BF)
    wo32 = jnp.zeros((16, LANES), F32)
    sub16 = lax.broadcasted_iota(jnp.int32, (16, LANES), 0)
    for j in range(CIN // 2):
        part = jnp.broadcast_to(
            wo_ref[0:1, LANES * j : LANES * j + LANES].astype(F32), (16, LANES)
        )
        wo32 = jnp.where(sub16 == 2 * j, part, wo32)
        wo32 = jnp.where(sub16 == 2 * j + 1, roll(part, CH), wo32)
    wo = wo32[:, 0:CH].astype(BF)
    wot = wo32.T[0:CH].astype(BF)
    zero64 = jnp.zeros((BS, BS), F32)
    one = interp_ref[...].astype(F32)
    matrix = jnp.concatenate(
        [jnp.concatenate([one, zero64], axis=1), jnp.concatenate([zero64, one], axis=1)], axis=0
    ).astype(BF)
    cot3 = cot_ref[...].astype(F32)
    cot = jnp.concatenate([cot3[:, q, :] for q in range(4)], axis=1).astype(BF)
    wanted = tgt_ref[...] & 511
    halves = jnp.concatenate([wanted >> 6, wanted & 63], axis=0).astype(F32).astype(BF)
    own_row = lax.broadcasted_iota(jnp.int32, (rows, nt), 0)
    own_peer = lax.broadcasted_iota(jnp.int32, (rows, nt), 1)
    copies = jnp.where((own_row // KC) % nt == own_peer, 1.0, 0.0).astype(BF)
    spots = lax.dot_general(
        copies, halves, (((1,), (1,)), ((), ())), preferred_element_type=F32
    )
    first_slot = lax.broadcasted_iota(jnp.int32, (rows, 1), 0) < nt * KC
    target = jnp.where(
        first_slot, spots[:, 0:1] * 64.0 + spots[:, 2:3], spots[:, 1:2] * 64.0 + spots[:, 3:4]
    ).astype(jnp.int32)

    def ex_copy(e, d, arrival):
        ok, device = neighbour(d)
        at = d if arrival else OPP[d]
        if d < 2:
            src = row_send.at[e, d]
            dst = row_recv.at[e, at]
        else:
            src = edge_send.at[e]
            dst = edge_recv.at[e, at - 2]
        return ok, pltpu.make_async_remote_copy(
            src_ref=src,
            dst_ref=dst,
            send_sem=ex_ssem.at[e, d],
            recv_sem=ex_rsem.at[e, at],
            device_id=device,
            device_id_type=MESH,
        )

    def wide_copy(e, i, arrival):
        d = i if i < 8 else i - 8
        ok, device = neighbour(d)
        at = d if arrival else OPP[d]
        if i >= 8:
            src = wide_own.at[e, 0 : WIDE_CH[e], LANES * d : LANES * d + 3 * LANES]
            dst = wide_recv.at[e, at, 0 : WIDE_CH[e]]
        else:
            src = rim_send.at[e]
            dst = rim_recv.at[e, at]
        return ok, pltpu.make_async_remote_copy(
            src_ref=src,
            dst_ref=dst,
            send_sem=wide_ssem.at[e, i],
            recv_sem=wide_rsem.at[e, at if i < 8 else 8 + at],
            device_id=device,
            device_id_type=MESH,
        )

    def start_all(copy_of, e, count):
        for d in reversed(range(count)):
            ok, copy = copy_of(e, d, False)
            pl.when(ok)(copy.start)

    def wait_all(copy_of, e, count):
        for d in range(count):
            ok, copy = copy_of(e, d, True)

            @pl.when(ok)
            def _(copy=copy):
                copy.wait_recv()
                copy.wait_send()

    lane16 = lanes_of(16)

    def edge_pick(rows_of):
        parts = []
        for targets in rows_of:
            right, left = sub16 < 0, sub16 < 0
            for j in targets:
                right, left = right | (sub16 == j), left | (sub16 == j + 8)
            hit = (right & (lane16 == LANES - 1)) | (left & (lane16 == 0))
            parts.append(jnp.where(hit, 1.0, 0.0))
        return jnp.concatenate(parts, axis=1).astype(BF)

    pick_coarse = edge_pick(((1, 2, 5), (0, 3, 4)))
    sub32 = lax.broadcasted_iota(jnp.int32, (32, LANES), 0)
    lane32 = lanes_of(32)
    column = sub32 & 7
    on_edge = ((column < 3) & (lane32 == column)) | (
        (column >= 3) & (column < 6) & (lane32 == LANES - 6 + column)
    )
    pick_rim = jnp.concatenate(
        [jnp.where(on_edge & ((sub32 >> 3) == r), 1.0, 0.0) for r in range(4)], axis=1
    ).astype(BF)

    def pick(table, field):
        return lax.dot_general(
            table, field, (((1,), (1,)), ((), ())), preferred_element_type=F32
        ).astype(BF)

    takes = {
        2: (sub16 >= 1) & (sub16 <= 4),
        3: (sub16 >= 9) & (sub16 <= 12),
        4: sub16 == 0,
        5: sub16 == 8,
        6: sub16 == 5,
        7: sub16 == 13,
    }

    def halo_columns(e):
        held = jnp.zeros((16, LANES), F32)
        for d in range(2, 8):
            held = jnp.where(takes[d], edge_recv[e, d - 2].astype(F32), held)
        return held.astype(BF)

    def place(columns, table):
        return lax.dot_general(
            columns, table, (((0,), (0,)), ((), ())), preferred_element_type=F32
        )

    def wide_start(e, own_rows):
        flat = jnp.concatenate(own_rows, axis=1)
        wide_own[e, 0 : WIDE_CH[e]] = flat
        rim_send[e, :, 0 : WIDE_CH[e]] = pick(pick_rim, flat)
        start_all(wide_copy, e, 10)

    def wide_finish(e, own_rows):
        wait_all(wide_copy, e, 10)
        rims = jnp.concatenate([rim_recv[e, d] for d in range(8)] + [rim_send[e]], axis=0)
        panel = place(rims, panel_ref[...])[0 : WIDE_CH[e]]
        above = [wide_recv[e, 0, 0 : WIDE_CH[e], LANES * r : LANES * r + LANES] for r in range(3)]
        below = [wide_recv[e, 1, 0 : WIDE_CH[e], LANES * r : LANES * r + LANES] for r in range(3)]
        return above + own_rows + below, panel

    def fill(x_ref, chans, offset, total, ext_rows, panel, row_lanes):
        count = len(ext_rows) - 2
        for a in range(3):
            at = slice(a * total + offset, a * total + offset + chans)
            for r in range(count):
                if ext_rows[r + a] is not None:
                    x_ref[at, r * LANES : (r + 1) * LANES] = ext_rows[r + a]
            if panel is not None:
                moved = roll(panel, (1 - a) * row_lanes) if a != 1 else panel
                x_ref[at, count * LANES :] = moved.astype(BF)

    side_lane = lanes_of(CH) & 63
    panel_row = ((side_lane * 43) >> 8) - 3
    panel_col = side_lane - (panel_row + 3) * PITCH
    on_right_side = lanes_of(CH) >= 64
    row_low = jnp.where(face > 0, -3, 0)
    row_high = jnp.where(face < nf - 1, 6, 3)
    left_low = jnp.where(tile > 0, 0, 3)
    right_high = jnp.where(tile < nt - 1, 5, 2)
    in_grid = (
        (panel_row >= row_low)
        & (panel_row <= row_high)
        & (on_right_side | (panel_col >= left_low))
        & (~on_right_side | (panel_col <= right_high))
    )

    groups = (
        (na, send_a, recv_a, part_a, zrecv_a, done_a, all_a, 0),
        (nb, send_b, recv_b, part_b, zrecv_b, done_b, all_b, 2),
        (nc, send_c, recv_c, part_c, zrecv_c, done_c, all_c, 0),
    )

    def xy_copy(g, k, arrival):
        other, device = xy_peer(k)
        send, recv, m = groups[g][1], groups[g][2], 16 * groups[g][0]
        at = other if arrival else me_xy
        return pltpu.make_async_remote_copy(
            src_ref=send.at[pl.ds(pl.multiple_of(other * m, 16), m)],
            dst_ref=recv.at[at],
            send_sem=xy_ssem.at[g, k],
            recv_sem=xy_rsem.at[g, at],
            device_id=device,
            device_id_type=MESH,
        )

    def xy_start(g):
        each(1, nxy, lambda k: xy_copy(g, k, False).start())

    def z_owner(g, q):
        return (4 * q + groups[g][7]) % nz

    def zs_copy(g, q, source):
        n, send, recv, part, zrecv, done, full, first = groups[g]
        base = 0 if g == 0 else na
        return pltpu.make_async_remote_copy(
            src_ref=part.at[16 * q : 16 * q + 16],
            dst_ref=zrecv.at[q, source],
            send_sem=zs_ssem.at[base + q],
            recv_sem=zs_rsem.at[base + q, source],
            device_id={"tile": y_hi * nz + z_owner(g, q)},
            device_id_type=MESH,
        )

    def zg_copy(g, q, k):
        n, send, recv, part, zrecv, done, full, first = groups[g]
        base = 0 if g == 0 else na
        return pltpu.make_async_remote_copy(
            src_ref=done.at[16 * q : 16 * q + 16],
            dst_ref=done.at[16 * q : 16 * q + 16],
            send_sem=zg_ssem.at[base + q, k],
            recv_sem=zg_rsem.at[base + q],
            device_id=z_peer(k)[1],
            device_id_type=MESH,
        )

    def gx_copy(g, k, arrival):
        other, device = xy_peer(k)
        n, send, recv, part, zrecv, done, full, first = groups[g]
        m = 16 * n
        at = other if arrival else me_xy
        return pltpu.make_async_remote_copy(
            src_ref=done,
            dst_ref=full.at[pl.ds(pl.multiple_of(at * m, 16), m)],
            send_sem=gx_ssem.at[g, k],
            recv_sem=gx_rsem.at[g, at],
            device_id=device,
            device_id_type=MESH,
        )

    def zall_copy(k, arrival):
        other, device = z_peer(k)
        return pltpu.make_async_remote_copy(
            src_ref=part_c,
            dst_ref=zrecv_c.at[other if arrival else z],
            send_sem=za_ssem.at[k],
            recv_sem=za_rsem.at[other if arrival else z],
            device_id=device,
            device_id_type=MESH,
        )

    def stage_all_z():
        each(1, nz, lambda k: zall_copy(k, True).wait_recv())
        zrecv_c[z] = part_c[...]
        total = zrecv_c[0].astype(F32)
        for j in range(1, nz):
            total = total + zrecv_c[j].astype(F32)
        done_c[...] = total.astype(BF)
        each(1, nxy, lambda k: gx_copy(2, k, False).start())

    def stage_xy_to_z(g):
        n, send, recv, part, zrecv, done, full, first = groups[g]
        m = 16 * n
        total = send[pl.ds(pl.multiple_of(me_xy * m, 16), m), :].astype(F32)
        each(1, nxy, lambda k: xy_copy(g, k, True).wait_recv())
        recv[me_xy] = jnp.zeros((m, LANES), BF)
        for j in range(nxy):
            total = total + recv[j].astype(F32)
        part[...] = total.astype(BF)
        if g == 2:
            each(1, nz, lambda k: zall_copy(k, False).start())
            return
        for q in range(n):

            @pl.when(z != z_owner(g, q))
            def _(q=q):
                zs_copy(g, q, z).start()

    def stage_z_reduce(g):
        n, send, recv, part, zrecv, done, full, first = groups[g]
        for q in range(n):

            @pl.when(z == z_owner(g, q))
            def _(q=q):
                each(1, nz, lambda k: zs_copy(g, q, z_peer(k)[0]).wait_recv())
                zrecv[q, z] = part[16 * q : 16 * q + 16]
                total = jnp.zeros((16, LANES), F32)
                for j in range(nz):
                    total = total + zrecv[q, j].astype(F32)
                done[16 * q : 16 * q + 16] = total.astype(BF)
                each(1, nz, lambda k: zg_copy(g, q, k).start())

    def stage_z_to_xy(g):
        n, send, recv, part, zrecv, done, full, first = groups[g]
        for q in range(n):

            @pl.when(z != z_owner(g, q))
            def _(q=q):
                zg_copy(g, q, 1).wait_recv()

        each(1, nxy, lambda k: gx_copy(g, k, False).start())

    def stage_finish(g):
        n, send, recv, part, zrecv, done, full, first = groups[g]
        m = 16 * n
        each(1, nxy, lambda k: gx_copy(g, k, True).wait_recv())
        full[pl.ds(pl.multiple_of(me_xy * m, 16), m), :] = done[...]
        each(1, nxy, lambda k: xy_copy(g, k, False).wait_send())
        each(1, nxy, lambda k: gx_copy(g, k, False).wait_send())
        if g == 2:
            each(1, nz, lambda k: zall_copy(k, False).wait_send())
            return
        for q in range(n):

            @pl.when(z != z_owner(g, q))
            def _(q=q):
                zs_copy(g, q, z).wait_send()

            @pl.when(z == z_owner(g, q))
            def _(q=q):
                each(1, nz, lambda k: zg_copy(g, q, k).wait_send())

    target = jnp.broadcast_to(target, (rows, LANES))
    shift_in = target & (LANES - 1)
    to_tile = (target >> 7) + (lane < shift_in).astype(jnp.int32)
    each(0, nt, lambda k: box_arrival(k).wait_recv())
    arrived = jnp.concatenate([inbox[p] for p in range(nt)], axis=0)
    moved = jnp.dot(arrived.astype(BF), matrix, preferred_element_type=F32)
    lane_half = lanes_of(rows // 2)
    moved = jnp.concatenate(
        [
            jnp.where(lane_half < BS, moved, 0.0),
            roll(jnp.where(lane_half >= BS, moved, 0.0), BS),
        ],
        axis=0,
    )
    moved = barrel(moved, shift_in, True)
    lifted = []
    for q in range(4):
        chosen = jnp.where(to_tile == q, moved, 0.0)
        total = chosen[0:8]
        for i in range(1, rows // 8):
            total = total + chosen[8 * i : 8 * i + 8]
        total = total + pltpu.roll(total, 4, axis=0)
        total = total * sea_ref[q : q + 1, :].astype(F32)
        forcing = jnp.concatenate(
            [jnp.where(sub8 < KC, total, 0.0), jnp.zeros((8, LANES), F32)], axis=0
        ).astype(BF)
        lifted.append(
            jnp.concatenate([state_rows[q].astype(BF), forcing], axis=0)
        )

    wide_start(0, lifted)
    ext, panel = wide_finish(0, lifted)
    fill(x1, 32, 0, 32, ext, panel, PITCH)
    pre, pre_panel = conv_rows(a1[...], x1, CH, 8, 1, lambda r: fine_lanes(r - 2))
    hidden_one, slope_one = [], []
    for r in range(8):
        value, slope = gelu_pair(pre[r])
        if r < 2:
            value = jnp.where(face > 0, value, 0.0)
        elif r >= 6:
            value = jnp.where(face < nf - 1, value, 0.0)
        else:
            slope_one.append(slope)
        hidden_one.append(value.astype(BF))
    one_panel = jnp.where(in_grid, gelu_pair(pre_panel)[0], 0.0).astype(BF).astype(F32)

    pooled = [
        (
            pair_sum(hidden_one[2 * r].astype(F32) + hidden_one[2 * r + 1].astype(F32)) * 0.25
        ).astype(BF)
        for r in range(4)
    ]

    def panel_sum(field):
        field = field + roll(field, -1)
        return field + roll(field, -PITCH)

    fill(x2, CH, 0, CH, pooled, panel_sum(one_panel) * 0.25, 2 * PITCH)
    pre, _ = conv_rows(a2[...], x2, 2 * CH, 2, 2, coarse_lanes)
    hidden_two, slope_two = [], []
    for r in range(2):
        value, slope = gelu_pair(pre[r])
        hidden_two.append(value.astype(BF))
        slope_two.append(slope)

    for e, field in ((0, hidden_two), (1, [slope.astype(BF) for slope in slope_two])):
        row_send[e, 0] = field[0]
        row_send[e, 1] = field[1]
        edge_send[e] = pick(pick_coarse, jnp.concatenate(field, axis=1))
        start_all(ex_copy, e, 8)
    fill(x3, CH, 0, 3 * CH, hidden_one[1:7], one_panel, PITCH)
    fill(x3, 2 * CH, CH, 3 * CH, [None] + [hidden_two[r // 2] for r in range(4)] + [None], None, 0)
    back_three = jnp.dot(wot, cot, preferred_element_type=F32)
    wait_all(ex_copy, 0, 8)
    columns = halo_columns(0)
    x3[CH : 3 * CH, 0:LANES] = row_recv[0, 0]
    x3[7 * CH : 9 * CH, 3 * LANES : 4 * LANES] = row_recv[0, 1]
    for a in range(3):
        x3[3 * CH * a + CH : 3 * CH * a + 3 * CH, 4 * LANES :] = place(
            columns, place_ref[a]
        ).astype(BF)
    pre, _ = conv_rows(a3[...], x3, CH, 4, 1, fine_lanes)
    hidden_three, delta_three = [], []
    for r in range(4):
        value, slope = gelu_pair(pre[r])
        hidden_three.append(value.astype(BF))
        delta_three.append(
            (back_three[:, r * LANES : (r + 1) * LANES] * slope).astype(BF)
        )

    wide_start(1, delta_three)
    flat_three = jnp.concatenate(hidden_three, axis=1)
    change = jnp.dot(wo, flat_three, preferred_element_type=F32)
    for r in range(4):
        pred32[:, r, :] = state_rows[r] + change[:, r * LANES : (r + 1) * LANES]
    pred_ref[...] = pred32[...].astype(BF)
    grad_out = lax.dot_general(
        cot, flat_three, (((1,), (1,)), ((), ())), preferred_element_type=F32
    )
    grad_up = weight_grad([d.astype(F32) for d in delta_three], x3[...], 1, fine_lanes)
    tiles = [grad_up[:, LANES * t : LANES * t + LANES] for t in range(4)]
    tiles.append(jnp.concatenate([grad_up[:, 512:576], jnp.zeros((192, CH), F32)], axis=1))
    lane_up = lanes_of(192)
    second = roll(tiles[2], CH)
    starts = (
        (tiles[0], tiles[1]),
        (jnp.where(lane_up < CH, roll(tiles[1], CH), second), second),
        (tiles[3], tiles[4]),
    )
    for a in range(3):
        for t in range(2):
            u3[3 * a, t] = starts[a][t][0:CH]
            u3[3 * a + 1, t] = starts[a][t][CH : 2 * CH]
            u3[3 * a + 2, t] = starts[a][t][2 * CH : 3 * CH]
    for k in range(9):
        even = [u3[k, t, pl.ds(0, CH // 2, stride=2), :] for t in range(2)]
        uneven = [roll(u3[k, t, pl.ds(1, CH // 2, stride=2), :], CH) for t in range(2)]
        pairs = (
            even[0],
            jnp.where(lane_j < CH, even[1], uneven[0]),
            jnp.where(lane_j < CH, uneven[0], uneven[1]),
        )
        for t in range(3):
            at = 32 * (9 * t + k)
            send_a[at : at + 32] = pairs[t].astype(BF)
    send_a[864:880] = jnp.concatenate([grad_out, jnp.zeros((16, 64), F32)], axis=1).astype(BF)
    if 16 * na * nxy > 880:
        send_a[880:] = jnp.zeros((16 * na * nxy - 880, LANES), BF)
    xy_start(0)
    wait_all(ex_copy, 1, 8)
    ext, panel = wide_finish(1, delta_three)
    fill(xd3, CH, 0, CH, ext, panel, PITCH)
    join, join_panel = conv_rows(b3[...], xd3, 3 * CH, 8, 1, lambda r: fine_lanes(r - 2))
    slopes = [row_recv[1, 0].astype(F32)] + slope_two + [row_recv[1, 1].astype(F32)]
    delta_two = [
        (pair_sum(join[2 * r][CH:] + join[2 * r + 1][CH:]) * slopes[r]).astype(BF)
        for r in range(4)
    ]
    two_panel = (
        (panel_sum(join_panel[CH:]) * place(halo_columns(1), place_ref[3])).astype(BF).astype(F32)
    )

    fill(xd2, 2 * CH, 0, 2 * CH, delta_two, two_panel, 2 * PITCH)
    grad_down = weight_grad([d.astype(F32) for d in delta_two[1:3]], x2[...], 2, coarse_lanes)
    lane_down = lanes_of(CH)
    right = jnp.concatenate([grad_down[:, 128:192], jnp.zeros((384, CH), F32)], axis=1)
    for b in range(3):
        u2[b] = grad_down[2 * CH * b : 2 * CH * b + 2 * CH, 0:LANES]
        u2[3 + b] = right[2 * CH * b : 2 * CH * b + 2 * CH]
    for b in range(3):
        for a in range(3):
            even = u2[3 * (a // 2) + b, pl.ds(0, CH, stride=2), :]
            uneven = u2[3 * (a // 2) + b, pl.ds(1, CH, stride=2), :]
            if a == 1:
                pair = jnp.where(lane_down < CH, roll(even, CH), uneven)
            else:
                pair = jnp.where(lane_down < CH, even, roll(uneven, CH))
            at = CH * (3 * a + b)
            send_b[at : at + CH] = pair.astype(BF)
    if 16 * nb * nxy > 576:
        send_b[576:] = jnp.zeros((16 * nb * nxy - 576, LANES), BF)
    xy_start(1)
    d_pool, _ = conv_rows(b2[...], xd2, CH, 2, 2, coarse_lanes)
    delta_one = [
        ((join[2 + r][0:CH] + 0.25 * d_pool[r // 2]) * slope_one[r]).astype(BF).astype(F32)
        for r in range(4)
    ]
    grad_first = weight_grad(
        delta_one,
        jnp.concatenate([x1[:, 2 * LANES : 6 * LANES], x1[:, 8 * LANES :]], axis=1),
        1,
        fine_lanes,
    )
    send_c[0:192] = jnp.concatenate([grad_first, jnp.zeros((192, 32), F32)], axis=1).astype(BF)
    if 16 * nc * nxy > 192:
        send_c[192:] = jnp.zeros((16 * nc * nxy - 192, LANES), BF)
    xy_start(2)
    stage_xy_to_z(0)
    stage_xy_to_z(1)
    stage_xy_to_z(2)
    stage_z_reduce(0)
    stage_z_reduce(1)
    stage_z_to_xy(0)
    stage_all_z()
    stage_z_to_xy(1)
    scale = 1.0 / math.sqrt(nf * 4 * nt * LANES)
    stage_finish(0)
    for t in range(3):
        for k in range(9):
            at = 32 * (9 * t + k)
            gup_ref[k, pl.ds(t, CH // 2, stride=3), :] = all_a[at : at + 32].astype(F32) * scale
    part = all_a[864:880].astype(F32) * scale
    turned = roll(part, CH)
    lane1 = lanes_of(1)
    for j in range(CIN // 2):
        gout_ref[j : j + 1] = jnp.where(
            lane1 < CH, part[2 * j : 2 * j + 1], turned[2 * j + 1 : 2 * j + 2]
        )
    stage_finish(2)
    sums = all_c[0:192].astype(F32)
    taps = jnp.concatenate(
        [
            roll(sums[CH * b : CH * b + CH], -32 * a) if a else sums[CH * b : CH * b + CH]
            for a in range(3)
            for b in range(3)
        ],
        axis=0,
    )
    taps = barrel(jnp.where(lane_first < CIN + KC, taps, 0.0), offset, True)
    flat_first = sum(
        lax.dot_general(
            find_ref[step],
            jnp.where((lane_first >= offset) == (step == 0), taps, 0.0).astype(BF),
            (((0,), (0,)), ((), ())),
            preferred_element_type=F32,
        )
        for step in range(2)
    )
    s1[...] = flat_first * scale
    for k in range(9):
        gfirst_ref[k] = s1[pl.ds(k, 10, stride=8), :] if k < 8 else s1[80:90]
    stage_finish(1)
    for k in range(9):
        gdown_ref[k] = all_b[CH * k : CH * k + CH].astype(F32) * scale
    each(0, nt, lambda k: box_copy(k).wait_send())


def local(
    nf,
    nt,
    state,
    cotangent,
    block_peer,
    source_start,
    target_start,
    interp,
    sea_mask,
    w_first,
    w_down,
    w_up,
    w_out,
):
    nxy, nz = nf * 2, nt // 2
    na, nb, nc = -(-55 // nxy), -(-36 // nxy), -(-12 // nxy)
    nblk = source_start.shape[-1]
    tables = [jnp.asarray(table, BF) for table in first_tables() + edge_tables()]
    operands = (
        state[0],
        cotangent[0],
        block_peer.reshape(1, nblk),
        source_start.reshape(1, nblk),
        target_start.reshape(nt, 2).T,
        interp[0],
        sea_mask[0],
        w_first[0],
        w_down[0],
        w_up[0],
        w_out,
        *tables,
    )
    dma = pltpu.SemaphoreType.DMA
    scratch = [pltpu.VMEM(op.shape, op.dtype) for op in operands]
    scratch += [
        dma((len(operands),)),
        pltpu.VMEM((LANES, LANES), F32),
        pltpu.VMEM((576, LANES), F32),
        pltpu.VMEM((3, 288, LANES), F32),
        pltpu.VMEM((9, 2 * CH, LANES), F32),
        pltpu.VMEM((9, 2, CH, LANES), F32),
        pltpu.VMEM((CIN, 4, LANES), F32),
        pltpu.VMEM((3 * CH, 96), BF),
        pltpu.VMEM((6 * CH, 3 * CH), BF),
        pltpu.VMEM((3 * CH, 9 * CH), BF),
        pltpu.VMEM((3 * CH, 6 * CH), BF),
        pltpu.VMEM((9 * CH, 3 * CH), BF),
        pltpu.VMEM((nt, KC, LANES), F32),
        pltpu.VMEM((nt, KC, LANES), F32),
        pltpu.VMEM((2, 2, LANES, LANES), BF),
        pltpu.VMEM((2, 2, LANES, LANES), BF),
        pltpu.VMEM((2, 16, LANES), BF),
        pltpu.VMEM((2, 6, 16, LANES), BF),
        pltpu.VMEM((2, CH, 4 * LANES), BF),
        pltpu.VMEM((2, 2, CH, 3 * LANES), BF),
        pltpu.VMEM((2, 32, LANES), BF),
        pltpu.VMEM((2, 8, 32, LANES), BF),
        pltpu.VMEM((96, 9 * LANES), BF),
        pltpu.VMEM((3 * CH, 3 * LANES), BF),
        pltpu.VMEM((9 * CH, 5 * LANES), BF),
        pltpu.VMEM((3 * CH, 9 * LANES), BF),
        pltpu.VMEM((6 * CH, 3 * LANES), BF),
    ]
    for n in (na, nb, nc):
        scratch += [
            pltpu.VMEM((nxy * n * 16, LANES), BF),
            pltpu.VMEM((nxy, n * 16, LANES), BF),
            pltpu.VMEM((n * 16, LANES), BF),
            pltpu.VMEM((nz, n * 16, LANES) if n == nc else (n, nz, 16, LANES), BF),
            pltpu.VMEM((n * 16, LANES), BF),
            pltpu.VMEM((nxy * n * 16, LANES), BF),
        ]
    scratch += [
        dma((nt,)),
        dma((nt,)),
        dma((2, 8)),
        dma((2, 8)),
        dma((2, 10)),
        dma((2, 10)),
        dma((3, nxy)),
        dma((3, nxy)),
        dma((na + nb,)),
        dma((na + nb, nz)),
        dma((na + nb, nz)),
        dma((na + nb,)),
        dma((3, nxy)),
        dma((3, nxy)),
        dma((nz,)),
        dma((nz,)),
    ]
    vmem = pl.BlockSpec(memory_space=pltpu.VMEM)
    predicted, grad_first, grad_down, grad_up, grad_out = pl.pallas_call(
        functools.partial(kernel, nf, nt, na, nb, nc),
        out_shape=(
            jax.ShapeDtypeStruct((CIN, 4, LANES), BF),
            jax.ShapeDtypeStruct((9, 10, LANES), F32),
            jax.ShapeDtypeStruct((9, 64, LANES), F32),
            jax.ShapeDtypeStruct((9, 96, LANES), F32),
            jax.ShapeDtypeStruct((8, LANES), F32),
        ),
        in_specs=[pl.BlockSpec(memory_space=pltpu.HBM)] * len(operands),
        out_specs=(vmem,) * 5,
        scratch_shapes=scratch,
        compiler_params=pltpu.CompilerParams(
            collective_id=0, has_side_effects=True, vmem_limit_bytes=64 * 2**20
        ),
    )(*operands)

    return (
        predicted[None],
        grad_first.reshape(1, 9, -1),
        grad_down.reshape(1, 9, -1),
        grad_up.reshape(1, 9, -1),
        grad_out.reshape(1, -1),
    )


def solution(mesh):
    return jax.shard_map(
        functools.partial(local, mesh.shape["face"], mesh.shape["tile"]),
        mesh=mesh,
        in_specs=(
            P("half", None, "face", "tile"),
            P("half", None, "face", "tile"),
            P("half", "face", "tile", None, None),
            P("half", "face", "tile", None),
            P("half", "face", "tile", None, None),
            P("half", None, None),
            P("half", "face", "tile"),
            P("half", None, None),
            P("half", None, None),
            P("half", None, None),
            P("half", None),
        ),
        out_specs=(
            P("half", None, "face", "tile"),
            P("half", None, None),
            P("half", None, None),
            P("half", None, None),
            P("half", None),
        ),
        check_vma=False,
    )
```
